256 devices in a mesh: dp: 64 (over x, z, y_hi), pipe: 4 (over y_lo, core).
Axes of the slice: x: 4, y: 4 (y_hi: 2, y_lo: 2; y = y_hi * 2 + y_lo), z: 8, core: 2. Of those that a mesh axis runs over, the one named last changes fastest.
Arguments:
- section_inputs: bfloat16 [4, 64, 2, 4, 8, 4, 256], P('pipe', 'dp'), may hold values from -3 to 3
- top_grad: bfloat16 [64, 2, 4, 8, 4, 256], P('dp'), may hold values from -6 to 6
- norm_gain: float32 [4, 256], P('pipe'), may hold values from 0.1 to 1.9
- norm_shift: float32 [4, 256], P('pipe'), may hold values from -3 to 3
- conv_weight: bfloat16 [4, 6912, 256], P('pipe', 'dp'), may hold values from -0.078125 to 0.078125
Outputs:
- input_grads: bfloat16 [4, 64, 2, 4, 8, 4, 256], P('pipe', 'dp')
- weight_grads: float32 [4, 6912, 256], P('pipe', 'dp')
The draws below stay inside these ranges and needn't reach their ends.
All inputs are finite; a program needn't handle non-finite values.
Results may differ from the reference program's by a relative error of at most 0.008.
Values may be sent and summed in bfloat16 or wider, within the bound.
No kernel may reach another device: no remote copies, remote signals or barrier semaphores. Data moves between devices by JAX's collectives and lax.ppermute only.
A program may use at most 64 MiB of HBM per device.

```python
import jax
import jax.numpy as jnp
from jax import lax

C = 256
GROUPS = 32
F = 4
H = 8
W = 4
M = 2
SECTIONS = 4
CLIPS = 64
N_PIPE = 4


def levels(key, dims, split, smallest, top_value):
    def one(axis_at, shards_of):
        steps = jax.random.uniform(jax.random.fold_in(jax.random.fold_in(key, 6), axis_at), (shards_of,), jnp.float32, smallest / len(split), top_value / len(split))
        return jnp.repeat(jnp.exp(steps), dims[axis_at] // shards_of).reshape((-1,) + (1,) * (len(dims) - axis_at - 1))

    gain = one(*split[0])
    for cut in split[1:]:
        gain = gain * one(*cut)
    return gain


def normal_values(own_key, extent, width, reach, cuts=(), dtype=jnp.bfloat16):
    values = jax.random.normal(own_key, extent, jnp.float32) * width
    if len(cuts) > 0:
        values = levels(own_key, extent, cuts, -0.22, 0.18) * values
    return jnp.clip(values, min=-reach, max=reach).astype(dtype)


def setup_inputs(seed: int = 0) -> dict:
    keys = jax.random.split(jax.random.key(seed), 6)
    section_inputs = normal_values(keys[0], (SECTIONS, CLIPS, M, F, H, W, C), 0.5, 3.0, ((0, 4), (1, 64)))
    top_grad = normal_values(keys[1], (CLIPS, M, F, H, W, C), 1.0, 6.0, ((0, 64),))
    norm_gain = jnp.clip(1.0 + 0.18 * jax.random.normal(keys[2], (SECTIONS, C), jnp.float32), 0.1, 1.9)
    norm_shift = normal_values(keys[3], (SECTIONS, C), 0.5, 3.0, ((0, 4),), jnp.float32)
    conv_weight = normal_values(keys[4], (SECTIONS, 27 * C, C), (27 * C) ** -0.5, 0.078125, ((0, 4), (1, 64)))
    return dict(section_inputs=section_inputs, top_grad=top_grad, norm_gain=norm_gain, norm_shift=norm_shift, conv_weight=conv_weight)


def norm_forward(x_float, gain_row, shift_row):
    dims_full = x_float.shape
    channels = dims_full[-1]
    grouped = x_float.reshape(dims_full[:-3] + (dims_full[-3] * dims_full[-2], GROUPS, channels // GROUPS))
    average = lax.optimization_barrier(jnp.mean(grouped, axis=(-3, -1), keepdims=True))
    variance = lax.optimization_barrier(jnp.mean(jnp.square(grouped - average), axis=(-3, -1), keepdims=True))
    inv_std = lax.rsqrt(variance + 1e-06)
    x_hat = ((grouped - average) * inv_std).reshape(dims_full)
    normed = x_hat * gain_row + shift_row
    return (normed, x_hat, inv_std)

def norm_backward(grad_act, normed, x_hat, inv_std, gain_row):
    sigmoid_n = jax.nn.sigmoid(normed)
    grad_hat = grad_act * sigmoid_n * (1.0 + normed * (1.0 - sigmoid_n)) * gain_row
    dims_full = grad_hat.shape
    grouped_shape = inv_std.shape[:-3] + (dims_full[-3] * dims_full[-2], GROUPS, dims_full[-1] // GROUPS)
    grad_grouped = grad_hat.reshape(grouped_shape)
    hat_grouped = x_hat.reshape(grouped_shape)
    first_mean = lax.optimization_barrier(jnp.mean(grad_grouped, axis=(-3, -1), keepdims=True))
    second_mean = lax.optimization_barrier(jnp.mean(grad_grouped * hat_grouped, axis=(-3, -1), keepdims=True))
    result = inv_std * (grad_grouped - first_mean - hat_grouped * second_mean)
    return result.reshape(dims_full)

def tap_offsets():
    return [(k_time, k_high, k_wide) for k_time in range(3) for k_high in range(3) for k_wide in range(3)]

def reference(section_inputs, top_grad, norm_gain, norm_shift, conv_weight):
    grad_now = top_grad
    input_list = []
    weight_list = []
    for section_idx in reversed(range(N_PIPE)):
        kernel = conv_weight[section_idx].reshape(27, C, C)
        gain_row = norm_gain[section_idx]
        shift_row = norm_shift[section_idx]

        def per_clip(carry, pair):
            x_clip, g_clip = pair
            normed, x_hat, inv_std = norm_forward(x_clip.astype(jnp.float32), gain_row, shift_row)
            acts = jax.nn.silu(normed).astype(jnp.bfloat16)
            g_pad = jnp.pad(g_clip, ((0, 0), (0, 2), (1, 1), (1, 1), (0, 0)))
            a_pad = jnp.pad(acts, ((0, 0), (2, 0), (1, 1), (1, 1), (0, 0)))
            grad_act = jnp.zeros((M * F * H * W, C), jnp.float32)
            flat_grad = g_clip.reshape(-1, C)
            tap_grads = []
            for tap_idx, (k_time, k_high, k_wide) in enumerate(tap_offsets()):
                g_slice = g_pad[:, 2 - k_time:2 - k_time + F, 2 - k_high:2 - k_high + H, 2 - k_wide:2 - k_wide + W]
                grad_act = grad_act + jnp.dot(g_slice.reshape(-1, C), kernel[tap_idx].T, preferred_element_type=jnp.float32)
                a_slice = a_pad[:, k_time:k_time + F, k_high:k_high + H, k_wide:k_wide + W].reshape(-1, C)
                tap_grads.append(lax.dot_general(a_slice, flat_grad, (((0,), (0,)), ((), ())), preferred_element_type=jnp.float32))
            grad_act = grad_act.reshape(M, F, H, W, C)
            grad_in = norm_backward(grad_act, normed, x_hat, inv_std, gain_row).astype(jnp.bfloat16)
            return (carry + jnp.stack(tap_grads, axis=0).reshape(27 * C, C), grad_in)
        zeros_dw = jnp.zeros((27 * C, C), jnp.float32)
        dw_total, grad_prev = lax.scan(per_clip, zeros_dw, (section_inputs[section_idx], grad_now))
        input_list.append(grad_prev)
        weight_list.append(dw_total / CLIPS)
        grad_now = grad_prev
    input_grads = jnp.stack(input_list[::-1], axis=0)
    weight_grads = jnp.stack(weight_list[::-1], axis=0)
    return (input_grads, weight_grads)
```

```python
import functools

import jax
import jax.numpy as jnp
import numpy as np
from jax import lax
from jax.experimental import pallas as pl
from jax.experimental.pallas import tpu as pltpu
from jax.sharding import Mesh, PartitionSpec as P

C = 256
F = 4
H = 8
W = 4
M = 2
HW = H * W
POS = M * F * HW
ROWS = 27 * C
NX, NZ, NYH = 4, 8, 2
PART = ROWS // (NX * NZ * NYH)
PAIR = NYH * PART
CHUNK = NZ * PAIR
HALF = CHUNK // 2
CLIPS = NX * NZ * NYH
BF = jnp.bfloat16
F32 = jnp.float32
HI = lax.Precision.HIGHEST
VMEM = pl.BlockSpec(memory_space=pltpu.VMEM)
SMEM = pl.BlockSpec(memory_space=pltpu.SMEM)
ANY = pl.BlockSpec(memory_space=pl.ANY)


def shift_matrices():
    s = np.zeros((9, C, C), np.float32)
    for kh in range(3):
        for kw in range(3):
            for h in range(H):
                for w in range(W):
                    h2, w2 = h - kh + 1, w - kw + 1
                    if 0 <= h2 < H and 0 <= w2 < W:
                        for f in range(C // HW):
                            s[kh * 3 + kw, f * HW + h * W + w, f * HW + h2 * W + w2] = 1
    return s


def group_matrix():
    c = np.arange(C) // 8
    return (c[:, None] == c[None, :]).astype(np.float32) / (8 * HW)


def spread(per_frame):
    frames = per_frame.shape[0]
    return jnp.broadcast_to(per_frame[:, None, :], (frames, HW, C)).reshape(frames * HW, C)


def frame_mean(value, group):
    sums = jnp.sum(value.reshape(-1, HW, C), axis=1)
    return jnp.dot(sums, group, precision=HI, preferred_element_type=F32)


def time_major(m, t):
    return (t * M + m) * HW


def plain(m, t):
    return (m * F + t) * HW


def forward_kernel(x_ref, gain_ref, shift_ref, group_ref, act_ref, xhat_ref, coef_ref, inv_ref, buf):
    for m in range(M):
        for t in range(F):
            buf[pl.ds(time_major(m, t), HW), :] = x_ref[pl.ds(plain(m, t), HW), :].astype(F32)
    group = group_ref[...]
    x = buf[...]
    centred = x - spread(frame_mean(x, group))
    inv = lax.rsqrt(frame_mean(centred * centred, group) + 1e-06)
    xhat = centred * spread(inv)
    gain = gain_ref[...]
    normed = xhat * gain + shift_ref[...]
    sig = jax.nn.sigmoid(normed)
    act_ref[...] = (normed * sig).astype(BF)
    xhat_ref[...] = xhat
    coef_ref[...] = sig * (1.0 + normed * (1.0 - sig)) * gain
    inv_ref[...] = inv


def forward(x, gain, shift, group):
    return pl.pallas_call(
        forward_kernel,
        out_shape=(
            jax.ShapeDtypeStruct((POS, C), BF),
            jax.ShapeDtypeStruct((POS, C), F32),
            jax.ShapeDtypeStruct((POS, C), F32),
            jax.ShapeDtypeStruct((POS // HW, C), F32),
        ),
        in_specs=[VMEM] * 4,
        out_specs=(VMEM,) * 4,
        scratch_shapes=[pltpu.VMEM((POS, C), F32)],
        compiler_params=pltpu.CompilerParams(vmem_limit_bytes=8 << 20),
        name="norm_forward",
    )(x, gain, shift, group)


def conv_kernel(
    flags, own, left, right, far_a, far_b, g_ref, s_ref, xhat_ref, coef_ref, inv_ref, group_ref,
    out_ref, kbuf, gs, sem,
):
    x = flags[0]
    pieces = (
        (own, x * CHUNK, CHUNK),
        (left, lax.rem(x + NX - 1, NX) * CHUNK, CHUNK),
        (right, lax.rem(x + 1, NX) * CHUNK, CHUNK),
        (far_a, lax.rem(x + 2, NX) * CHUNK, HALF),
        (far_b, lax.rem(x + 2, NX) * CHUNK + HALF, HALF),
    )
    copies = [
        pltpu.make_async_copy(ref, kbuf.at[pl.ds(pl.multiple_of(at, 32), rows), :], sem.at[i])
        for i, (ref, at, rows) in enumerate(pieces)
    ]
    for copy in copies:
        copy.start()
    g = g_ref[...]
    for j in range(9):
        gs[j, pl.ds(0, POS), :] = jnp.dot(
            s_ref[j], g, preferred_element_type=F32
        ).astype(BF)
        gs[j, pl.ds(POS, 2 * M * HW), :] = jnp.zeros((2 * M * HW, C), BF)
    for copy in copies:
        copy.wait()
    grad_act = None
    for kt in range(3):
        for j in range(9):
            term = lax.dot_general(
                gs[j, pl.ds((2 - kt) * M * HW, POS), :],
                kbuf[pl.ds((kt * 9 + j) * C, C), :],
                (((1,), (1,)), ((), ())),
                preferred_element_type=F32,
            )
            grad_act = term if grad_act is None else grad_act + term
    group = group_ref[...]
    xhat = xhat_ref[...]
    grad_hat = grad_act * coef_ref[...]
    first = spread(frame_mean(grad_hat, group))
    second = spread(frame_mean(grad_hat * xhat, group))
    out_ref[...] = (spread(inv_ref[...]) * (grad_hat - first - xhat * second)).astype(BF)


def conv_back(flags, pieces, g, s, xhat, coef, inv, group):
    return pl.pallas_call(
        conv_kernel,
        out_shape=jax.ShapeDtypeStruct((POS, C), BF),
        in_specs=[SMEM] + [ANY] * 5 + [VMEM] * 6,
        out_specs=VMEM,
        scratch_shapes=[
            pltpu.VMEM((ROWS, C), BF),
            pltpu.VMEM((9, POS + 2 * M * HW, C), BF),
            pltpu.SemaphoreType.DMA((5,)),
        ],
        compiler_params=pltpu.CompilerParams(vmem_limit_bytes=24 << 20),
        cost_estimate=pl.CostEstimate(flops=2 * POS * ROWS * C, bytes_accessed=2 * ROWS * C, transcendentals=0),
        name="conv_back",
    )(flags, *pieces, g, s, xhat, coef, inv, group)


def columns_kernel(flags, own, left, right, far_a, far_b, s_ref, at_ref, turned):
    blocks = ((own, 0), (own, 1), (left, 0), (left, 1), (right, 0), (right, 1), (far_a, None), (far_b, None))
    for t in range(2):
        turned[t] = jnp.zeros((C, C), BF)
    for t in range(F):
        rows = [
            ref[pl.ds(t * HW if m is None else time_major(m, t), HW), :] for ref, m in blocks
        ]
        turned[t + 2] = jnp.concatenate(rows, axis=0).astype(F32).T.astype(BF)
    first = lax.div(flags[0] * (CHUNK // 64), 4)
    for k in range(8):
        tap = jnp.minimum(first + k, 26)
        kt = lax.div(tap, 9)
        j = lax.rem(tap, 9)
        moved = s_ref[j]
        for t in range(F):
            at_ref[pl.ds(k * C, C), pl.ds(t * C, C)] = jnp.dot(
                turned[t + kt], moved, preferred_element_type=F32
            ).astype(BF)


def columns(flags, acts, s):
    return pl.pallas_call(
        columns_kernel,
        out_shape=jax.ShapeDtypeStruct((8 * C, F * C), BF),
        in_specs=[SMEM] + [VMEM] * 6,
        out_specs=VMEM,
        scratch_shapes=[pltpu.VMEM((F + 2, C, C), BF)],
        compiler_params=pltpu.CompilerParams(vmem_limit_bytes=24 << 20),
        name="act_columns",
    )(flags, *acts, s)


def weight_kernel(flags, at_ref, own, left, right, far_a, far_b, out_ref, part, gbuf, sem):
    x = flags[0]
    offset = lax.rem(x * (CHUNK // 64), 4) * 64
    steps = CHUNK // (2 * PAIR)
    copies = [
        pltpu.make_async_copy(
            at_ref.at[pl.ds(pl.multiple_of(offset + i * 2 * PAIR, 16), 2 * PAIR), :], part.at[i], sem.at[i]
        )
        for i in range(steps)
    ]
    for copy in copies:
        copy.start()
    blocks = ((own, 0), (own, 1), (left, 0), (left, 1), (right, 0), (right, 1), (far_a, None), (far_b, None))
    for t in range(F):
        for b, (ref, m) in enumerate(blocks):
            gbuf[pl.ds(t * C + b * HW, HW), :] = ref[pl.ds(t * HW if m is None else time_major(m, t), HW), :]
    for i in range(steps):
        copies[i].wait()
        total = jnp.dot(part[i], gbuf[...], preferred_element_type=F32)
        out_ref[2 * i] = total[:PAIR].astype(BF)
        out_ref[2 * i + 1] = total[PAIR:].astype(BF)


def weight_back(flags, at, grads):
    steps = CHUNK // (2 * PAIR)
    return pl.pallas_call(
        weight_kernel,
        out_shape=jax.ShapeDtypeStruct((NZ, PAIR, C), BF),
        in_specs=[SMEM, ANY] + [VMEM] * 5,
        out_specs=VMEM,
        scratch_shapes=[
            pltpu.VMEM((steps, 2 * PAIR, F * C), BF),
            pltpu.VMEM((F * C, C), BF),
            pltpu.SemaphoreType.DMA((steps,)),
        ],
        compiler_params=pltpu.CompilerParams(vmem_limit_bytes=16 << 20),
        cost_estimate=pl.CostEstimate(flops=2 * CHUNK * F * C * C, bytes_accessed=6 << 20, transcendentals=0),
        name="weight_back",
    )(flags, at, *grads)


def ring(axis, step):
    n = lax.axis_size(axis)
    return [(i, (i + step) % n) for i in range(n)]


def gather_x(block, first_half, second_half):
    left = lax.ppermute(block, "x", ring("x", 1))
    right = lax.ppermute(block, "x", ring("x", -1))
    far_a = lax.ppermute(first_half(left), "x", ring("x", 1))
    far_b = lax.ppermute(second_half(right), "x", ring("x", -1))
    return block, left, right, far_a, far_b


def to_time_major(value):
    return value.reshape(M, F, HW, C).transpose(1, 0, 2, 3).reshape(POS, C)


def halves_of_clip():
    def pick(m):
        return lambda b: b.reshape(F, M, HW, C)[:, m].reshape(F * HW, C)

    return pick(0), pick(1)


def local(section_inputs, top_grad, norm_gain, norm_shift, conv_weight):
    s = jnp.asarray(shift_matrices(), BF)
    group = jnp.asarray(group_matrix(), F32)
    x_at = lax.axis_index("x")
    yh = lax.axis_index("yh")
    section = lax.axis_index("yl") * 2 + lax.axis_index("c")
    flags = x_at.astype(jnp.int32).reshape(1)

    rows = conv_weight[0]
    other = lax.ppermute(rows, "yh", ring("yh", 1))
    pair = jnp.where(yh == 0, jnp.concatenate([rows, other]), jnp.concatenate([other, rows]))
    chunk = lax.all_to_all(
        jnp.broadcast_to(pair[None], (NZ, PAIR, C)), "z", 0, 0, tiled=True
    ).reshape(CHUNK, C)
    kernel_pieces = gather_x(chunk, lambda b: b[:HALF], lambda b: b[HALF:])

    act, xhat, coef, inv = forward(section_inputs.reshape(POS, C), norm_gain, norm_shift, group)
    at = columns(flags, gather_x(act, *halves_of_clip()), s)

    g = to_time_major(top_grad.reshape(POS, C))
    for k in range(3):
        sent = conv_back(flags, kernel_pieces, g, s, xhat, coef, inv, group)
        src, dst = 3 - k, 2 - k
        arrived = lax.ppermute(sent, ("yl", "c"), [(src, dst)])
        g = jnp.where(section == dst, arrived, g)
    grads = gather_x(g, *halves_of_clip())
    dx = conv_back(flags, kernel_pieces, g, s, xhat, coef, inv, group)

    partial = weight_back(flags, at, grads)
    summed = jnp.sum(lax.all_to_all(partial, "z", 0, 0, tiled=True).astype(F32), axis=0)
    low, high = summed[:PART], summed[PART:]
    arrived = lax.ppermute(jnp.where(yh == 0, high, low), "yh", ring("yh", 1))
    weight_part = (jnp.where(yh == 0, low, high) + arrived) * (1.0 / CLIPS)

    dx = dx.reshape(F, M, HW, C).transpose(1, 0, 2, 3).reshape(section_inputs.shape)
    return dx, weight_part[None]


def solution(mesh):
    fine = Mesh(mesh.devices.reshape(NX, NZ, NYH, 2, 2), ("x", "z", "yh", "yl", "c"))
    dp, pipe = ("x", "z", "yh"), ("yl", "c")
    placed = (
        P(pipe, dp, None, None, None, None, None),
        P(dp, None, None, None, None, None),
        P(pipe, None),
        P(pipe, None),
        P(pipe, dp, None),
    )
    return jax.shard_map(
        local,
        mesh=fine,
        in_specs=placed,
        out_specs=(P(pipe, dp, None, None, None, None, None), P(pipe, dp, None)),
        check_vma=False,
    )
```

```python
import jax
import jax.numpy as jnp
import numpy as np
from jax import lax
from jax.experimental import pallas as pl
from jax.experimental.pallas import tpu as pltpu
from jax.sharding import Mesh, PartitionSpec as P

C = 256
F = 4
H = 8
W = 4
M = 2
HW = H * W
POS = M * F * HW
ROWS = 27 * C
NX, NZ, NYH = 4, 8, 2
N_PIPE = 4
PART = ROWS // (NX * NZ * NYH)
PAIR = NYH * PART
CHUNK = NZ * PAIR
HC = C // NYH
SLOTS = NZ * HC
CLIPS = NX * NZ * NYH
GRANT = 24 << 20
BF = jnp.bfloat16
F32 = jnp.float32
HI = lax.Precision.HIGHEST
VMEM = pl.BlockSpec(memory_space=pltpu.VMEM)
SMEM = pl.BlockSpec(memory_space=pltpu.SMEM)
HBM = pl.BlockSpec(memory_space=pltpu.HBM)


def shift_matrices():
    s = np.zeros((9, HC, HC), np.float32)
    for kh in range(3):
        for kw in range(3):
            for h in range(H):
                for w in range(W):
                    h2, w2 = h - kh + 1, w - kw + 1
                    if 0 <= h2 < H and 0 <= w2 < W:
                        for f in range(HC // HW):
                            s[kh * 3 + kw, f * HW + h * W + w, f * HW + h2 * W + w2] = 1
    return s


def group_matrix(channels):
    row = lax.div(lax.broadcasted_iota(jnp.int32, (channels, channels), 0), 8)
    column = lax.div(lax.broadcasted_iota(jnp.int32, (channels, channels), 1), 8)
    return jnp.where(row == column, 1.0 / (8 * HW), 0.0).astype(F32)


def spread(per_frame):
    frames, channels = per_frame.shape
    return jnp.broadcast_to(per_frame[:, None, :], (frames, HW, channels)).reshape(frames * HW, channels)


def frame_mean(value, group):
    sums = jnp.sum(value.reshape(-1, HW, value.shape[-1]), axis=1)
    return jnp.dot(sums, group, precision=HI, preferred_element_type=F32)


def time_major(m, t):
    return (t * M + m) * HW


def plain(m, t):
    return (m * F + t) * HW


def normalise(x, group):
    centred = x - spread(frame_mean(x, group))
    inv = lax.rsqrt(frame_mean(centred * centred, group) + 1e-06)
    return centred * spread(inv), inv


def forward_kernel(x_ref, gain_ref, shift_ref, act_ref, buf):
    for m in range(M):
        for t in range(F):
            buf[pl.ds(time_major(m, t), HW), :] = x_ref[pl.ds(plain(m, t), HW), :].astype(F32)
    xhat, _ = normalise(buf[...], group_matrix(C))
    normed = xhat * gain_ref[...] + shift_ref[...]
    act_ref[...] = (normed * jax.nn.sigmoid(normed)).astype(BF)


def forward(x, gain, shift):
    return pl.pallas_call(
        forward_kernel,
        out_shape=jax.ShapeDtypeStruct((POS, C), BF),
        in_specs=[VMEM] * 3,
        out_specs=VMEM,
        scratch_shapes=[pltpu.VMEM((POS, C), F32)],
        compiler_params=pltpu.CompilerParams(vmem_limit_bytes=GRANT),
        name="norm_forward",
    )(x, gain, shift)


def pair_row(k, m, t):
    return ((t * NYH + k) * M + m) * HW


def factors_kernel(flags, mine, theirs, gain_ref, shift_ref, out_ref, buf):
    first = flags[1] == 0
    for m in range(M):
        for t in range(F):
            a = mine[pl.ds(plain(m, t), HW), :].astype(F32)
            b = theirs[pl.ds(plain(m, t), HW), :].astype(F32)
            buf[pl.ds(pair_row(0, m, t), HW), :] = jnp.where(first, a, b)
            buf[pl.ds(pair_row(1, m, t), HW), :] = jnp.where(first, b, a)
    xhat, inv = normalise(buf[...], group_matrix(HC))
    gain = gain_ref[...]
    normed = xhat * gain + shift_ref[...]
    sig = jax.nn.sigmoid(normed)
    out_ref[0] = xhat
    out_ref[1] = sig * (1.0 + normed * (1.0 - sig)) * gain
    out_ref[2] = spread(inv)


def factors(flags, mine, theirs, gain, shift):
    return pl.pallas_call(
        factors_kernel,
        out_shape=jax.ShapeDtypeStruct((3, NYH * POS, HC), F32),
        in_specs=[SMEM] + [VMEM] * 4,
        out_specs=VMEM,
        scratch_shapes=[pltpu.VMEM((NYH * POS, HC), F32)],
        compiler_params=pltpu.CompilerParams(vmem_limit_bytes=GRANT),
        name="norm_factors",
    )(flags, mine, theirs, gain, shift)


def conv_kernel(
    flags, same, cross, s_ref, own, left, right, far_a, far_b, fac_ref,
    out_ref, kbuf, fac, gs, krows, sem,
):
    x = flags[0]
    yh = flags[1]
    rows = NYH * POS
    pieces = (
        (own, x * SLOTS, SLOTS),
        (left, lax.rem(x + NX - 1, NX) * SLOTS, SLOTS),
        (right, lax.rem(x + 1, NX) * SLOTS, SLOTS),
        (far_a, lax.rem(x + 2, NX) * SLOTS, SLOTS // 2),
        (far_b, lax.rem(x + 2, NX) * SLOTS + SLOTS // 2, SLOTS // 2),
    )
    later = [
        pltpu.make_async_copy(ref, kbuf.at[pl.ds(pl.multiple_of(at, HC), size), :], sem.at[i])
        for i, (ref, at, size) in enumerate(pieces)
    ]
    last = pltpu.make_async_copy(fac_ref, fac, sem.at[5])
    for copy in later + [last]:
        copy.start()
    kept, got = same[...], cross[...]
    g = jnp.concatenate([jnp.where(yh == 0, kept, got), jnp.where(yh == 0, got, kept)], axis=1)
    for j in range(9):
        for r in range(rows // HC):
            gs[pl.ds(r * HC, HC), pl.ds(j * C, C)] = jnp.dot(
                s_ref[j], g[r * HC : (r + 1) * HC], preferred_element_type=F32
            ).astype(BF)
    for copy in later:
        copy.wait()
    slot = lax.broadcasted_iota(jnp.int32, (HC, C), 0)
    for kt in range(3):
        for j in range(9):
            row = (kt * 9 + j) * C + yh * HC
            window = lax.div(row, PAIR)
            after = jnp.minimum(window + 1, NX * NZ - 1)
            here = kbuf[pl.ds(pl.multiple_of(window * HC, HC), HC), :]
            there = kbuf[pl.ds(pl.multiple_of(after * HC, HC), HC), :]
            krows[pl.ds(kt * HC, HC), pl.ds(j * C, C)] = jnp.where(
                slot < (window + 1) * PAIR - row, here, there
            )
    product = lax.dot_general(
        gs[...], krows[...], (((1,), (1,)), ((), ())), preferred_element_type=F32
    )
    frame = rows // F
    grad_act = product[:, 2 * HC :]
    for kt in range(2):
        ahead = (2 - kt) * frame
        part = product[ahead:, kt * HC : (kt + 1) * HC]
        grad_act = grad_act + jnp.concatenate([part, jnp.zeros((ahead, HC), F32)], axis=0)
    last.wait()
    xhat = fac[0]
    grad_hat = grad_act * fac[1]
    sums = jnp.concatenate(
        [jnp.sum(v.reshape(-1, HW, HC), axis=1) for v in (grad_hat, grad_hat * xhat)], axis=0
    )
    means = jnp.dot(sums, group_matrix(HC), precision=HI, preferred_element_type=F32)
    frames = rows // HW
    result = fac[2] * (grad_hat - spread(means[:frames]) - xhat * spread(means[frames:]))
    out_ref[...] = result.astype(BF)


def conv_back(flags, g, s, pieces, fac):
    rows = NYH * POS
    return pl.pallas_call(
        conv_kernel,
        out_shape=jax.ShapeDtypeStruct((rows, HC), BF),
        in_specs=[SMEM] + [VMEM] * 3 + [HBM] * 6,
        out_specs=VMEM,
        scratch_shapes=[
            pltpu.VMEM((NX * SLOTS, C), BF),
            pltpu.VMEM((3, rows, HC), F32),
            pltpu.VMEM((rows, 9 * C), BF),
            pltpu.VMEM((3 * HC, 9 * C), BF),
            pltpu.SemaphoreType.DMA((6,)),
        ],
        compiler_params=pltpu.CompilerParams(vmem_limit_bytes=GRANT),
        cost_estimate=pl.CostEstimate(flops=2 * POS * ROWS * C, bytes_accessed=ROWS * C, transcendentals=0),
        name="conv_back",
    )(flags, *g, s, *pieces, fac)


def columns_kernel(flags, own, left, right, far_a, far_b, s_ref, at_ref, turned):
    blocks = ((own, 0), (own, 1), (left, 0), (left, 1), (right, 0), (right, 1), (far_a, None), (far_b, None))
    for t in range(2):
        turned[t] = jnp.zeros((C, C), BF)
    for t in range(F):
        rows = [
            ref[pl.ds(t * HW if m is None else time_major(m, t), HW), :] for ref, m in blocks
        ]
        turned[t + 2] = jnp.concatenate(rows, axis=0).astype(F32).T.astype(BF)
    first = lax.div(flags[0] * (CHUNK // 64), 4)
    for k in range(8):
        tap = jnp.minimum(first + k, 26)
        kt = lax.div(tap, 9)
        j = lax.rem(tap, 9)
        moved = s_ref[j]
        for t in range(F):
            for r in range(C // HC):
                at_ref[pl.ds(k * C, C), pl.ds(t * C + r * HC, HC)] = jnp.dot(
                    turned[t + kt, :, pl.ds(r * HC, HC)], moved, preferred_element_type=F32
                ).astype(BF)


def columns(flags, acts, s):
    return pl.pallas_call(
        columns_kernel,
        out_shape=jax.ShapeDtypeStruct((8 * C, F * C), BF),
        in_specs=[SMEM] + [VMEM] * 6,
        out_specs=VMEM,
        scratch_shapes=[pltpu.VMEM((F + 2, C, C), BF)],
        compiler_params=pltpu.CompilerParams(vmem_limit_bytes=GRANT),
        name="act_columns",
    )(flags, *acts, s)


def weight_kernel(flags, at_ref, own, left, right, far_a, far_b, out_ref, gbuf):
    offset = lax.rem(flags[0] * (CHUNK // 64), 4) * 64
    blocks = ((own, 0), (own, 1), (left, 0), (left, 1), (right, 0), (right, 1), (far_a, None), (far_b, None))
    for t in range(F):
        for b, (ref, m) in enumerate(blocks):
            gbuf[pl.ds(t * C + b * HW, HW), :] = ref[pl.ds(t * HW if m is None else time_major(m, t), HW), :]
    for i in range(CHUNK // (2 * PAIR)):
        rows = at_ref[pl.ds(pl.multiple_of(offset + i * 2 * PAIR, 16), 2 * PAIR), :]
        total = jnp.dot(rows, gbuf[...], preferred_element_type=F32) * (1.0 / CLIPS)
        for k in range(4):
            out_ref[4 * i + k] = total[k * PART : (k + 1) * PART].astype(BF)


def weight_back(flags, at, grads):
    return pl.pallas_call(
        weight_kernel,
        out_shape=jax.ShapeDtypeStruct((NZ * NYH, PART, C), BF),
        in_specs=[SMEM] + [VMEM] * 6,
        out_specs=VMEM,
        scratch_shapes=[pltpu.VMEM((F * C, C), BF)],
        compiler_params=pltpu.CompilerParams(vmem_limit_bytes=GRANT),
        cost_estimate=pl.CostEstimate(flops=2 * CHUNK * F * C * C, bytes_accessed=6 << 20, transcendentals=0),
        name="weight_back",
    )(flags, at, *grads)


def ring(axis, step):
    n = lax.axis_size(axis)
    return [(i, (i + step) % n) for i in range(n)]


def gather_x(block, first_half, second_half, between=None):
    left = lax.ppermute(block, "x", ring("x", 1))
    right = lax.ppermute(block, "x", ring("x", -1))
    if between is not None:
        left, right, between = lax.optimization_barrier((left, right, between))
    far_a = lax.ppermute(first_half(left), "x", ring("x", 1))
    far_b = lax.ppermute(second_half(right), "x", ring("x", -1))
    blocks = (block, left, right, far_a, far_b)
    return blocks if between is None else (blocks, between)


def halves_of_clip():
    def pick(m):
        return lambda b: b.reshape(F, M, HW, C)[:, m].reshape(F * HW, C)

    return pick(0), pick(1)


def local(section_inputs, top_grad, norm_gain, norm_shift, conv_weight):
    s = jnp.asarray(shift_matrices(), BF)
    x_at = lax.axis_index("x")
    yh = lax.axis_index("yh")
    dp = (x_at * NZ + lax.axis_index("z")) * NYH + yh
    section = lax.axis_index("yl") * 2 + lax.axis_index("c")
    flags = jnp.stack([x_at, yh]).astype(jnp.int32)
    swap = ring("yh", 1)

    def mine(value, axis):
        return lax.dynamic_slice_in_dim(value, yh * HC, HC, axis)

    def theirs(value, axis):
        return lax.dynamic_slice_in_dim(value, (1 - yh) * HC, HC, axis)

    def in_order(kept, got, axis):
        return jnp.concatenate([jnp.where(yh == 0, kept, got), jnp.where(yh == 0, got, kept)], axis=axis)

    channel = lax.rem(dp * PART + lax.broadcasted_iota(jnp.int32, (C, PART), 1), C)
    place = (channel == lax.broadcasted_iota(jnp.int32, (C, PART), 0)).astype(BF)
    slots = jnp.dot(place, conv_weight[0], preferred_element_type=F32).astype(BF)
    window = mine(slots, 0) + lax.ppermute(theirs(slots, 0), "yh", swap)
    x_in = section_inputs.reshape(POS, C)
    act = forward(x_in, norm_gain, norm_shift)
    window, act = lax.optimization_barrier((window, act))
    chunk = lax.all_to_all(
        jnp.broadcast_to(window[None], (NZ, HC, C)), "z", 0, 0, tiled=True
    ).reshape(SLOTS, C)
    fac = factors(
        flags, mine(x_in, 1), lax.ppermute(theirs(x_in, 1), "yh", swap),
        mine(norm_gain, 1), mine(norm_shift, 1),
    )

    top = top_grad.reshape(M, F, HW, C).transpose(1, 0, 2, 3).reshape(F, 1, M * HW, C)
    both = in_order(top, lax.ppermute(top, "yh", swap), 1).reshape(NYH * POS, C)
    arrived = (mine(both, 1), theirs(both, 1))
    kernel_rows, (arrived, fac) = gather_x(
        chunk, lambda b: b[: SLOTS // 2], lambda b: b[SLOTS // 2 :], (arrived, fac)
    )
    own_g = top.reshape(POS, C)
    pair_dx = None
    for k in range(4):
        if k > 0:
            two = [lax.dynamic_index_in_dim(v.reshape(F, NYH, M * HW, HC), yh, 1, False) for v in arrived]
            own_g = jnp.where(section == 3 - k, in_order(*two, -1).reshape(POS, C), own_g)
        sent = conv_back(flags, arrived, s, kernel_rows, fac)
        if k == 0:
            sent, act = lax.optimization_barrier((sent, act))
            acts = gather_x(act, *halves_of_clip())
        pair_dx = sent if k == 0 else jnp.where(section == 3 - k, sent, pair_dx)
        if k < 3:
            src, dst = 3 - k, 2 - k
            cross = lax.ppermute(
                sent, ("yh", "yl", "c"), [(y * N_PIPE + src, (1 - y) * N_PIPE + dst) for y in range(NYH)]
            )
            arrived = (lax.ppermute(sent, ("yl", "c"), [(src, dst)]), cross)

    own_g, acts = lax.optimization_barrier((own_g, acts))
    at = columns(flags, acts, s)
    partial = weight_back(flags, at, gather_x(own_g, *halves_of_clip()))
    weight_part = jnp.sum(lax.all_to_all(partial, ("z", "yh"), 0, 0, tiled=True).astype(F32), axis=0)

    pair_dx = pair_dx.reshape(F, NYH, M, HW, HC)
    kept = lax.dynamic_index_in_dim(pair_dx, yh, 1, False)
    got = lax.ppermute(lax.dynamic_index_in_dim(pair_dx, 1 - yh, 1, False), "yh", swap)
    dx = in_order(kept, got, -1).transpose(1, 0, 2, 3).reshape(section_inputs.shape)
    return dx, weight_part[None]


def solution(mesh):
    fine = Mesh(mesh.devices.reshape(NX, NZ, NYH, 2, 2), ("x", "z", "yh", "yl", "c"))
    dp, pipe = ("x", "z", "yh"), ("yl", "c")
    placed = (
        P(pipe, dp, None, None, None, None, None),
        P(dp, None, None, None, None, None),
        P(pipe, None),
        P(pipe, None),
        P(pipe, dp, None),
    )
    return jax.shard_map(
        local,
        mesh=fine,
        in_specs=placed,
        out_specs=(P(pipe, dp, None, None, None, None, None), P(pipe, dp, None)),
        check_vma=False,
    )
```

```python
import functools

import jax
import jax.numpy as jnp
import numpy as np
from jax import lax
from jax.experimental import pallas as pl
from jax.experimental.pallas import tpu as pltpu
from jax.sharding import Mesh, PartitionSpec as P

C = 256
F = 4
H = 8
W = 4
M = 2
HW = H * W
POS = M * F * HW
ROWS = 27 * C
NX, NZ, NYH = 4, 8, 2
N_PIPE = 4
PART = ROWS // (NX * NZ * NYH)
PAIR = NYH * PART
CHUNK = NZ * PAIR
HC = C // NYH
WIDE = 2 * NX * M * HW
SLOTS = NZ * HC
CLIPS = NX * NZ * NYH
GRANT = 24 << 20
BF = jnp.bfloat16
F32 = jnp.float32
HI = lax.Precision.HIGHEST
VMEM = pl.BlockSpec(memory_space=pltpu.VMEM)
SMEM = pl.BlockSpec(memory_space=pltpu.SMEM)
HBM = pl.BlockSpec(memory_space=pltpu.HBM)


def shift_matrices(size):
    s = np.zeros((9, size, size), np.float32)
    for kh in range(3):
        for kw in range(3):
            for h in range(H):
                for w in range(W):
                    h2, w2 = h - kh + 1, w - kw + 1
                    if 0 <= h2 < H and 0 <= w2 < W:
                        for f in range(size // HW):
                            s[kh * 3 + kw, f * HW + h * W + w, f * HW + h2 * W + w2] = 1
    return s


def group_matrix(channels):
    row = lax.div(lax.broadcasted_iota(jnp.int32, (channels, channels), 0), 8)
    column = lax.div(lax.broadcasted_iota(jnp.int32, (channels, channels), 1), 8)
    return jnp.where(row == column, 1.0 / (8 * HW), 0.0).astype(F32)


def spread(per_frame):
    frames, channels = per_frame.shape
    return jnp.broadcast_to(per_frame[:, None, :], (frames, HW, channels)).reshape(frames * HW, channels)


def frame_mean(value, group):
    sums = jnp.sum(value.reshape(-1, HW, value.shape[-1]), axis=1)
    return jnp.dot(sums, group, precision=HI, preferred_element_type=F32)


def time_major(m, t):
    return (t * M + m) * HW


def plain(m, t):
    return (m * F + t) * HW


def normalise(x, group):
    centred = x - spread(frame_mean(x, group))
    inv = lax.rsqrt(frame_mean(centred * centred, group) + 1e-06)
    return centred * spread(inv), inv


def forward_kernel(x_ref, gain_ref, shift_ref, act_ref, buf):
    for m in range(M):
        for t in range(F):
            buf[pl.ds(time_major(m, t), HW), :] = x_ref[pl.ds(plain(m, t), HW), :].astype(F32)
    xhat, _ = normalise(buf[...], group_matrix(C))
    normed = xhat * gain_ref[...] + shift_ref[...]
    act_ref[...] = (normed * jax.nn.sigmoid(normed)).astype(BF)


def forward(x, gain, shift):
    return pl.pallas_call(
        forward_kernel,
        out_shape=jax.ShapeDtypeStruct((POS, C), BF),
        in_specs=[VMEM] * 3,
        out_specs=VMEM,
        scratch_shapes=[pltpu.VMEM((POS, C), F32)],
        compiler_params=pltpu.CompilerParams(vmem_limit_bytes=GRANT),
        name="norm_forward",
    )(x, gain, shift)


def pair_row(k, m, t):
    return ((t * NYH + k) * M + m) * HW


def factors_kernel(flags, mine, theirs, gain_ref, shift_ref, out_ref, buf):
    first = flags[1] == 0
    for m in range(M):
        for t in range(F):
            a = mine[pl.ds(plain(m, t), HW), :].astype(F32)
            b = theirs[pl.ds(plain(m, t), HW), :].astype(F32)
            buf[pl.ds(pair_row(0, m, t), HW), :] = jnp.where(first, a, b)
            buf[pl.ds(pair_row(1, m, t), HW), :] = jnp.where(first, b, a)
    xhat, inv = normalise(buf[...], group_matrix(HC))
    gain = gain_ref[...]
    normed = xhat * gain + shift_ref[...]
    sig = jax.nn.sigmoid(normed)
    out_ref[0] = xhat
    out_ref[1] = sig * (1.0 + normed * (1.0 - sig)) * gain
    out_ref[2] = spread(inv)


def factors(flags, mine, theirs, gain, shift):
    return pl.pallas_call(
        factors_kernel,
        out_shape=jax.ShapeDtypeStruct((3, NYH * POS, HC), F32),
        in_specs=[SMEM] + [VMEM] * 4,
        out_specs=VMEM,
        scratch_shapes=[pltpu.VMEM((NYH * POS, HC), F32)],
        compiler_params=pltpu.CompilerParams(vmem_limit_bytes=GRANT),
        name="norm_factors",
    )(flags, mine, theirs, gain, shift)


def conv_kernel(target, flags, *refs):
    @pl.when(flags[2] == target)
    def _():
        conv_body(flags, *refs)


def conv_body(
    flags, same, cross, s_ref, own, left, right, far_a, far_b, fac_ref,
    out_ref, kbuf, fac, gs, krows, sem,
):
    x = flags[0]
    yh = flags[1]
    rows = NYH * POS
    pieces = (
        (own, x * SLOTS, SLOTS),
        (left, lax.rem(x + NX - 1, NX) * SLOTS, SLOTS),
        (right, lax.rem(x + 1, NX) * SLOTS, SLOTS),
        (far_a, lax.rem(x + 2, NX) * SLOTS, SLOTS // 2),
        (far_b, lax.rem(x + 2, NX) * SLOTS + SLOTS // 2, SLOTS // 2),
    )
    later = [
        pltpu.make_async_copy(ref, kbuf.at[pl.ds(pl.multiple_of(at, HC), size), :], sem.at[i])
        for i, (ref, at, size) in enumerate(pieces)
    ]
    last = pltpu.make_async_copy(fac_ref, fac, sem.at[5])
    for copy in later + [last]:
        copy.start()
    kept, got = same[...], cross[...]
    g = jnp.concatenate([jnp.where(yh == 0, kept, got), jnp.where(yh == 0, got, kept)], axis=1)
    for j in range(9):
        for r in range(rows // HC):
            gs[pl.ds(r * HC, HC), pl.ds(j * C, C)] = jnp.dot(
                s_ref[j], g[r * HC : (r + 1) * HC], preferred_element_type=F32
            ).astype(BF)
    for copy in later:
        copy.wait()
    slot = lax.broadcasted_iota(jnp.int32, (HC, C), 0)
    for kt in range(3):
        for j in range(9):
            row = (kt * 9 + j) * C + yh * HC
            window = lax.div(row, PAIR)
            after = jnp.minimum(window + 1, NX * NZ - 1)
            here = kbuf[pl.ds(pl.multiple_of(window * HC, HC), HC), :]
            there = kbuf[pl.ds(pl.multiple_of(after * HC, HC), HC), :]
            krows[pl.ds(kt * HC, HC), pl.ds(j * C, C)] = jnp.where(
                slot < (window + 1) * PAIR - row, here, there
            )
    product = lax.dot_general(
        gs[...], krows[...], (((1,), (1,)), ((), ())), preferred_element_type=F32
    )
    frame = rows // F
    grad_act = product[:, 2 * HC :]
    for kt in range(2):
        ahead = (2 - kt) * frame
        part = product[ahead:, kt * HC : (kt + 1) * HC]
        grad_act = grad_act + jnp.concatenate([part, jnp.zeros((ahead, HC), F32)], axis=0)
    last.wait()
    xhat = fac[0]
    grad_hat = grad_act * fac[1]
    sums = jnp.concatenate(
        [jnp.sum(v.reshape(-1, HW, HC), axis=1) for v in (grad_hat, grad_hat * xhat)], axis=0
    )
    means = jnp.dot(sums, group_matrix(HC), precision=HI, preferred_element_type=F32)
    frames = rows // HW
    result = fac[2] * (grad_hat - spread(means[:frames]) - xhat * spread(means[frames:]))
    out_ref[...] = result.astype(BF)


def conv_back(target, flags, g, s, pieces, fac):
    rows = NYH * POS
    return pl.pallas_call(
        functools.partial(conv_kernel, target),
        out_shape=jax.ShapeDtypeStruct((rows, HC), BF),
        in_specs=[SMEM] + [VMEM] * 3 + [HBM] * 6,
        out_specs=VMEM,
        scratch_shapes=[
            pltpu.VMEM((NX * SLOTS, C), BF),
            pltpu.VMEM((3, rows, HC), F32),
            pltpu.VMEM((rows, 9 * C), BF),
            pltpu.VMEM((3 * HC, 9 * C), BF),
            pltpu.SemaphoreType.DMA((6,)),
        ],
        compiler_params=pltpu.CompilerParams(vmem_limit_bytes=GRANT),
        cost_estimate=pl.CostEstimate(flops=2 * POS * ROWS * C, bytes_accessed=ROWS * C, transcendentals=0),
        name="conv_back",
    )(flags, *g, s, *pieces, fac)


def rows_at(t, blocks):
    own, left, right, far_a, far_b = blocks
    pair, clip = NYH * M * HW, M * HW
    return [ref[pl.ds(t * pair, pair), :] for ref in (own, left, right)] + [
        ref[pl.ds(t * clip, clip), :] for ref in (far_a, far_b)
    ]


def weight_kernel(
    flags, own, left, right, far_a, far_b, g_own, g_left, g_right, g_far_a, g_far_b, s_ref,
    out_ref, a_own, a_left, a_right, a_far_a, a_far_b, shifts, turned, at, gbuf, sem,
):
    yh = flags[1]
    acts = (a_own, a_left, a_right, a_far_a, a_far_b)
    copies = [
        pltpu.make_async_copy(src, dst, sem.at[i])
        for i, (src, dst) in enumerate(
            zip((own, left, right, far_a, far_b, s_ref), acts + (shifts,))
        )
    ]
    for copy in copies:
        copy.start()
    for t in range(F):
        gbuf[pl.ds(t * WIDE, WIDE), :] = jnp.concatenate(
            rows_at(t, (g_own, g_left, g_right, g_far_a, g_far_b)), axis=0
        )
    turned[pl.ds(0, 2)] = jnp.zeros((2, C, WIDE), BF)
    for copy in copies:
        copy.wait()
    for t in range(F):
        rows = jnp.concatenate(rows_at(t, acts), axis=0)
        turned[t + 2] = rows.astype(F32).T.astype(BF)
    first = lax.div(flags[0] * (CHUNK // 64), 4)
    for k in range(8):
        tap = jnp.minimum(first + k, 26)
        kt = lax.div(tap, 9)
        moved = shifts[lax.rem(tap, 9)]
        for t in range(F):
            for r in range(WIDE // C):
                at[pl.ds(k * C, C), pl.ds(t * WIDE + r * C, C)] = jnp.dot(
                    turned[t + kt, :, pl.ds(r * C, C)], moved, preferred_element_type=F32
                ).astype(BF)
    offset = lax.rem(flags[0] * (CHUNK // 64), 4) * 64
    for z in range(NZ):
        skip = [(z * PAIR + k * PART) % 16 for k in range(NYH)]
        start = offset + jnp.where(yh == 0, z * PAIR - skip[0], z * PAIR + PART - skip[1])
        total = jnp.dot(
            at[pl.ds(pl.multiple_of(start, 16), HC), :], gbuf[...], preferred_element_type=F32
        ) * (1.0 / CLIPS)
        out_ref[z] = jnp.where(
            yh == 0, total[skip[0] : skip[0] + PART], total[skip[1] : skip[1] + PART]
        ).astype(BF)


def weight_back(flags, acts, grads, s):
    pieces = [pltpu.VMEM(v.shape, BF) for v in acts]
    return pl.pallas_call(
        weight_kernel,
        out_shape=jax.ShapeDtypeStruct((NZ, PART, C), BF),
        in_specs=[SMEM] + [HBM] * 5 + [VMEM] * 5 + [HBM],
        out_specs=VMEM,
        scratch_shapes=pieces
        + [
            pltpu.VMEM((9, C, C), BF),
            pltpu.VMEM((F + 2, C, WIDE), BF),
            pltpu.VMEM((8 * C, F * WIDE), BF),
            pltpu.VMEM((F * WIDE, C), BF),
            pltpu.SemaphoreType.DMA((6,)),
        ],
        compiler_params=pltpu.CompilerParams(vmem_limit_bytes=GRANT),
        cost_estimate=pl.CostEstimate(flops=2 * CHUNK * F * C * C, bytes_accessed=6 << 20, transcendentals=0),
        name="weight_back",
    )(flags, *acts, *grads, s)


def ring(axis, step):
    n = lax.axis_size(axis)
    return [(i, (i + step) % n) for i in range(n)]


def gather_x(block, first_half, second_half, between=None):
    left = lax.ppermute(block, "x", ring("x", 1))
    right = lax.ppermute(block, "x", ring("x", -1))
    if between is not None:
        left, right, between = lax.optimization_barrier((left, right, between))
    far_a = lax.ppermute(first_half(left), "x", ring("x", 1))
    far_b = lax.ppermute(second_half(right), "x", ring("x", -1))
    blocks = (block, left, right, far_a, far_b)
    return blocks if between is None else (blocks, between)


def clips_of_pair():
    def pick(k):
        return lambda b: b.reshape(F, NYH, M * HW, C)[:, k].reshape(POS, C)

    return pick(0), pick(1)


def local(section_inputs, top_grad, norm_gain, norm_shift, conv_weight):
    s = jnp.asarray(shift_matrices(HC), BF)
    wide_s = jnp.asarray(shift_matrices(C), BF)
    x_at = lax.axis_index("x")
    yh = lax.axis_index("yh")
    dp = (x_at * NZ + lax.axis_index("z")) * NYH + yh
    section = lax.axis_index("yl") * 2 + lax.axis_index("c")
    flags = jnp.stack([x_at, yh, section]).astype(jnp.int32)
    swap = ring("yh", 1)

    def mine(value, axis):
        return lax.dynamic_slice_in_dim(value, yh * HC, HC, axis)

    def theirs(value, axis):
        return lax.dynamic_slice_in_dim(value, (1 - yh) * HC, HC, axis)

    def in_order(kept, got, axis):
        return jnp.concatenate([jnp.where(yh == 0, kept, got), jnp.where(yh == 0, got, kept)], axis=axis)

    channel = lax.rem(dp * PART + lax.broadcasted_iota(jnp.int32, (C, PART), 1), C)
    place = (channel == lax.broadcasted_iota(jnp.int32, (C, PART), 0)).astype(BF)
    slots = jnp.dot(place, conv_weight[0], preferred_element_type=F32).astype(BF)
    window = mine(slots, 0) + lax.ppermute(theirs(slots, 0), "yh", swap)
    x_in = section_inputs.reshape(POS, C)
    act = forward(x_in, norm_gain, norm_shift)
    window, act = lax.optimization_barrier((window, act))
    chunk = lax.all_to_all(
        jnp.broadcast_to(window[None], (NZ, HC, C)), "z", 0, 0, tiled=True
    ).reshape(SLOTS, C)
    fac = factors(
        flags, mine(x_in, 1), lax.ppermute(theirs(x_in, 1), "yh", swap),
        mine(norm_gain, 1), mine(norm_shift, 1),
    )

    top = top_grad.reshape(M, F, HW, C).transpose(1, 0, 2, 3).reshape(F, 1, M * HW, C)
    both = in_order(top, lax.ppermute(top, "yh", swap), 1).reshape(NYH * POS, C)
    arrived = (mine(both, 1), theirs(both, 1))
    act = act.reshape(F, 1, M * HW, C)
    act = in_order(act, lax.ppermute(act, "yh", swap), 1).reshape(NYH * POS, C)
    kernel_rows, (arrived, fac, act) = gather_x(
        chunk, lambda b: b[: SLOTS // 2], lambda b: b[SLOTS // 2 :], (arrived, fac, act)
    )
    pair_g = both
    pair_dx = None
    for k in range(4):
        if k > 0:
            pair_g = jnp.where(section == 3 - k, in_order(*arrived, 1), pair_g)
        sent = conv_back(3 - k, flags, arrived, s, kernel_rows, fac)
        if k == 0:
            sent, act = lax.optimization_barrier((sent, act))
            acts = gather_x(act, *clips_of_pair())
        pair_dx = sent if k == 0 else jnp.where(section == 3 - k, sent, pair_dx)
        if k < 3:
            src, dst = 3 - k, 2 - k
            same = lax.ppermute(sent, ("yl", "c"), [(src, dst)])
            cross = lax.ppermute(
                sent, ("yh", "yl", "c"), [(y * N_PIPE + src, (1 - y) * N_PIPE + dst) for y in range(NYH)]
            )
            arrived = (same, cross)

    pair_dx = pair_dx.reshape(F, NYH, M, HW, HC)
    kept = lax.dynamic_index_in_dim(pair_dx, yh, 1, False)
    given = lax.dynamic_index_in_dim(pair_dx, 1 - yh, 1, False)
    grads, (kept, given) = gather_x(pair_g, *clips_of_pair(), (kept, given))
    got = lax.ppermute(given, "yh", swap)
    dx = in_order(kept, got, -1).transpose(1, 0, 2, 3).reshape(section_inputs.shape)

    partial = weight_back(flags, acts, grads, wide_s)
    weight_part = jnp.sum(lax.all_to_all(partial, "z", 0, 0, tiled=True).astype(F32), axis=0)
    return dx, weight_part[None]


def solution(mesh):
    fine = Mesh(mesh.devices.reshape(NX, NZ, NYH, 2, 2), ("x", "z", "yh", "yl", "c"))
    dp, pipe = ("x", "z", "yh"), ("yl", "c")
    placed = (
        P(pipe, dp, None, None, None, None, None),
        P(dp, None, None, None, None, None),
        P(pipe, None),
        P(pipe, None),
        P(pipe, dp, None),
    )
    return jax.shard_map(
        local,
        mesh=fine,
        in_specs=placed,
        out_specs=(P(pipe, dp, None, None, None, None, None), P(pipe, dp, None)),
        check_vma=False,
    )
```

```python
import functools

import jax
import jax.numpy as jnp
import numpy as np
from jax import lax
from jax.experimental import pallas as pl
from jax.experimental.pallas import tpu as pltpu
from jax.sharding import Mesh, PartitionSpec as P

C = 256
F = 4
H = 8
W = 4
M = 2
HW = H * W
POS = M * F * HW
ROWS = 27 * C
NX, NZ, NYH = 4, 8, 2
N_PIPE = 4
PART = ROWS // (NX * NZ * NYH)
PAIR = NYH * PART
CHUNK = NZ * PAIR
HC = C // NYH
SLOTS = NZ * HC
CLIPS = NX * NZ * NYH
GRANT = 24 << 20
BF = jnp.bfloat16
F32 = jnp.float32
HI = lax.Precision.HIGHEST
VMEM = pl.BlockSpec(memory_space=pltpu.VMEM)
SMEM = pl.BlockSpec(memory_space=pltpu.SMEM)
HBM = pl.BlockSpec(memory_space=pltpu.HBM)


def shift_matrices(size):
    s = np.zeros((9, size, size), np.float32)
    for kh in range(3):
        for kw in range(3):
            for h in range(H):
                for w in range(W):
                    h2, w2 = h - kh + 1, w - kw + 1
                    if 0 <= h2 < H and 0 <= w2 < W:
                        for f in range(size // HW):
                            s[kh * 3 + kw, f * HW + h * W + w, f * HW + h2 * W + w2] = 1
    return s


def group_matrix(channels):
    row = lax.div(lax.broadcasted_iota(jnp.int32, (channels, channels), 0), 8)
    column = lax.div(lax.broadcasted_iota(jnp.int32, (channels, channels), 1), 8)
    return jnp.where(row == column, 1.0 / (8 * HW), 0.0).astype(F32)


def spread(per_frame):
    frames, channels = per_frame.shape
    return jnp.broadcast_to(per_frame[:, None, :], (frames, HW, channels)).reshape(frames * HW, channels)


def frame_mean(value, group):
    sums = jnp.sum(value.reshape(-1, HW, value.shape[-1]), axis=1)
    return jnp.dot(sums, group, precision=HI, preferred_element_type=F32)


def time_major(m, t):
    return (t * M + m) * HW


def plain(m, t):
    return (m * F + t) * HW


def normalise(x, group):
    centred = x - spread(frame_mean(x, group))
    inv = lax.rsqrt(frame_mean(centred * centred, group) + 1e-06)
    return centred * spread(inv), inv


def forward_kernel(x_ref, gain_ref, shift_ref, act_ref, buf):
    for m in range(M):
        for t in range(F):
            buf[pl.ds(time_major(m, t), HW), :] = x_ref[pl.ds(plain(m, t), HW), :].astype(F32)
    xhat, _ = normalise(buf[...], group_matrix(C))
    normed = xhat * gain_ref[...] + shift_ref[...]
    act_ref[...] = (normed * jax.nn.sigmoid(normed)).astype(BF)


def forward(x, gain, shift):
    return pl.pallas_call(
        forward_kernel,
        out_shape=jax.ShapeDtypeStruct((POS, C), BF),
        in_specs=[VMEM] * 3,
        out_specs=VMEM,
        scratch_shapes=[pltpu.VMEM((POS, C), F32)],
        compiler_params=pltpu.CompilerParams(vmem_limit_bytes=GRANT),
        name="norm_forward",
    )(x, gain, shift)


def pair_row(k, m, t):
    return ((t * NYH + k) * M + m) * HW


def factors_kernel(flags, mine, theirs, gain_ref, shift_ref, out_ref, buf):
    first = flags[1] == 0
    for m in range(M):
        for t in range(F):
            a = mine[pl.ds(plain(m, t), HW), :].astype(F32)
            b = theirs[pl.ds(plain(m, t), HW), :].astype(F32)
            buf[pl.ds(pair_row(0, m, t), HW), :] = jnp.where(first, a, b)
            buf[pl.ds(pair_row(1, m, t), HW), :] = jnp.where(first, b, a)
    xhat, inv = normalise(buf[...], group_matrix(HC))
    gain = gain_ref[...]
    normed = xhat * gain + shift_ref[...]
    sig = jax.nn.sigmoid(normed)
    out_ref[0] = xhat
    out_ref[1] = sig * (1.0 + normed * (1.0 - sig)) * gain
    out_ref[2] = spread(inv)


def factors(flags, mine, theirs, gain, shift):
    return pl.pallas_call(
        factors_kernel,
        out_shape=jax.ShapeDtypeStruct((3, NYH * POS, HC), F32),
        in_specs=[SMEM] + [VMEM] * 4,
        out_specs=VMEM,
        scratch_shapes=[pltpu.VMEM((NYH * POS, HC), F32)],
        compiler_params=pltpu.CompilerParams(vmem_limit_bytes=GRANT),
        name="norm_factors",
    )(flags, mine, theirs, gain, shift)


def conv_kernel(target, flags, *refs):
    @pl.when(flags[2] == target)
    def _():
        conv_body(flags, *refs)


def conv_body(
    flags, same, cross, s_ref, own, left, right, far_a, far_b, fac_ref,
    out_ref, kbuf, fac, gs, krows, sem,
):
    x = flags[0]
    yh = flags[1]
    rows = NYH * POS
    pieces = (
        (own, x * SLOTS, SLOTS),
        (left, lax.rem(x + NX - 1, NX) * SLOTS, SLOTS),
        (right, lax.rem(x + 1, NX) * SLOTS, SLOTS),
        (far_a, lax.rem(x + 2, NX) * SLOTS, SLOTS // 2),
        (far_b, lax.rem(x + 2, NX) * SLOTS + SLOTS // 2, SLOTS // 2),
    )
    later = [
        pltpu.make_async_copy(ref, kbuf.at[pl.ds(pl.multiple_of(at, HC), size), :], sem.at[i])
        for i, (ref, at, size) in enumerate(pieces)
    ]
    last = pltpu.make_async_copy(fac_ref, fac, sem.at[5])
    for copy in later + [last]:
        copy.start()
    kept, got = same[...], cross[...]
    g = jnp.concatenate([jnp.where(yh == 0, kept, got), jnp.where(yh == 0, got, kept)], axis=1)
    for j in range(9):
        for r in range(rows // HC):
            gs[pl.ds(r * HC, HC), pl.ds(j * C, C)] = jnp.dot(
                s_ref[j], g[r * HC : (r + 1) * HC], preferred_element_type=F32
            ).astype(BF)
    for copy in later:
        copy.wait()
    slot = lax.broadcasted_iota(jnp.int32, (HC, C), 0)
    for kt in range(3):
        for j in range(9):
            row = (kt * 9 + j) * C + yh * HC
            window = lax.div(row, PAIR)
            after = jnp.minimum(window + 1, NX * NZ - 1)
            here = kbuf[pl.ds(pl.multiple_of(window * HC, HC), HC), :]
            there = kbuf[pl.ds(pl.multiple_of(after * HC, HC), HC), :]
            krows[pl.ds(kt * HC, HC), pl.ds(j * C, C)] = jnp.where(
                slot < (window + 1) * PAIR - row, here, there
            )
    product = lax.dot_general(
        gs[...], krows[...], (((1,), (1,)), ((), ())), preferred_element_type=F32
    )
    frame = rows // F
    grad_act = product[:, 2 * HC :]
    for kt in range(2):
        ahead = (2 - kt) * frame
        part = product[ahead:, kt * HC : (kt + 1) * HC]
        grad_act = grad_act + jnp.concatenate([part, jnp.zeros((ahead, HC), F32)], axis=0)
    last.wait()
    xhat = fac[0]
    grad_hat = grad_act * fac[1]
    sums = jnp.concatenate(
        [jnp.sum(v.reshape(-1, HW, HC), axis=1) for v in (grad_hat, grad_hat * xhat)], axis=0
    )
    means = jnp.dot(sums, group_matrix(HC), precision=HI, preferred_element_type=F32)
    frames = rows // HW
    result = fac[2] * (grad_hat - spread(means[:frames]) - xhat * spread(means[frames:]))
    out_ref[...] = result.astype(BF)


def conv_back(target, flags, g, s, pieces, fac):
    rows = NYH * POS
    return pl.pallas_call(
        functools.partial(conv_kernel, target),
        out_shape=jax.ShapeDtypeStruct((rows, HC), BF),
        in_specs=[SMEM] + [VMEM] * 3 + [HBM] * 6,
        out_specs=VMEM,
        scratch_shapes=[
            pltpu.VMEM((NX * SLOTS, C), BF),
            pltpu.VMEM((3, rows, HC), F32),
            pltpu.VMEM((rows, 9 * C), BF),
            pltpu.VMEM((3 * HC, 9 * C), BF),
            pltpu.SemaphoreType.DMA((6,)),
        ],
        compiler_params=pltpu.CompilerParams(vmem_limit_bytes=GRANT),
        cost_estimate=pl.CostEstimate(flops=2 * POS * ROWS * C, bytes_accessed=ROWS * C, transcendentals=0),
        name="conv_back",
    )(flags, *g, s, *pieces, fac)


def weight_kernel(count, tail, *refs):
    flags, acts, grads, (s_ref, *before, out_ref) = (
        refs[0], refs[1 : 1 + count], refs[1 + count : 1 + 2 * count], refs[1 + 2 * count : -4 - count]
    )
    held, (turned, at, gbuf, sem) = refs[-4 - count : -4], refs[-4:]
    yh = flags[1]
    copies = [pltpu.make_async_copy(src, dst, sem.at[i]) for i, (src, dst) in enumerate(zip(acts, held))]
    for copy in copies:
        copy.start()
    wide = gbuf.shape[0] // F

    def frame(blocks, t):
        rows = blocks[0].shape[0] // F
        return jnp.concatenate([ref[pl.ds(t * rows, rows), :] for ref in blocks], axis=0)

    for t in range(F):
        gbuf[pl.ds(t * wide, wide), :] = frame(grads, t)
    turned[pl.ds(0, 2)] = jnp.zeros((2, C, wide), BF)
    for copy in copies:
        copy.wait()
    for t in range(F):
        turned[t + 2] = frame(held, t).astype(F32).T.astype(BF)
    first = lax.div(flags[0] * (CHUNK // 64), 4)
    for k in range(8):
        tap = jnp.minimum(first + k, 26)
        kt = lax.div(tap, 9)
        j = lax.rem(tap, 9)
        for t in range(F):
            for at_lane in range(0, wide, C):
                size = min(C, wide - at_lane)
                moved = s_ref[j, :size, :size]
                at[pl.ds(k * C, C), pl.ds(t * wide + at_lane, size)] = jnp.dot(
                    turned[t + kt, :, pl.ds(at_lane, size)], moved, preferred_element_type=F32
                ).astype(BF)
    offset = lax.rem(flags[0] * (CHUNK // 64), 4) * 64
    for z in range(NZ):
        skip = [(z * PAIR + k * PART) % 16 for k in range(NYH)]
        start = offset + jnp.where(yh == 0, z * PAIR - skip[0], z * PAIR + PART - skip[1])
        total = jnp.dot(
            at[pl.ds(pl.multiple_of(start, 16), HC), :], gbuf[...], preferred_element_type=F32
        )
        if before:
            total = total + before[0][z]
        if tail:
            total = total * (1.0 / CLIPS)
            total = jnp.where(yh == 0, total[skip[0] : skip[0] + PART], total[skip[1] : skip[1] + PART])
        out_ref[z] = total.astype(out_ref.dtype)


def weight_back(flags, acts, grads, s, before=None):
    tail = before is not None
    wide = sum(v.shape[0] // F for v in acts)
    return pl.pallas_call(
        functools.partial(weight_kernel, len(acts), tail),
        out_shape=jax.ShapeDtypeStruct((NZ, PART if tail else HC, C), BF if tail else F32),
        in_specs=[SMEM] + [HBM] * len(acts) + [VMEM] * len(grads) + [VMEM] * (1 + tail),
        out_specs=VMEM,
        scratch_shapes=[pltpu.VMEM(v.shape, BF) for v in acts]
        + [
            pltpu.VMEM((F + 2, C, wide), BF),
            pltpu.VMEM((8 * C, F * wide), BF),
            pltpu.VMEM((F * wide, C), BF),
            pltpu.SemaphoreType.DMA((len(acts),)),
        ],
        compiler_params=pltpu.CompilerParams(vmem_limit_bytes=GRANT),
        cost_estimate=pl.CostEstimate(
            flops=8 * CHUNK * wide * C, bytes_accessed=4 << 20, transcendentals=0
        ),
        name="weight_last" if tail else "weight_first",
    )(flags, *acts, *grads, s, *([before] if tail else []))


def ring(axis, step):
    n = lax.axis_size(axis)
    return [(i, (i + step) % n) for i in range(n)]


def gather_x(block, first_half, second_half, between=None):
    left = lax.ppermute(block, "x", ring("x", 1))
    right = lax.ppermute(block, "x", ring("x", -1))
    if between is not None:
        left, right, between = lax.optimization_barrier((left, right, between))
    far_a = lax.ppermute(first_half(left), "x", ring("x", 1))
    far_b = lax.ppermute(second_half(right), "x", ring("x", -1))
    blocks = (block, left, right, far_a, far_b)
    return blocks if between is None else (blocks, between)


def clips_of_pair():
    def pick(k):
        return lambda b: b.reshape(F, NYH, M * HW, C)[:, k].reshape(POS, C)

    return pick(0), pick(1)


def local(section_inputs, top_grad, norm_gain, norm_shift, conv_weight):
    s = jnp.asarray(shift_matrices(HC), BF)
    wide_s = jnp.asarray(shift_matrices(C), BF)
    x_at = lax.axis_index("x")
    yh = lax.axis_index("yh")
    dp = (x_at * NZ + lax.axis_index("z")) * NYH + yh
    section = lax.axis_index("yl") * 2 + lax.axis_index("c")
    flags = jnp.stack([x_at, yh, section]).astype(jnp.int32)
    swap = ring("yh", 1)

    def mine(value, axis):
        return lax.dynamic_slice_in_dim(value, yh * HC, HC, axis)

    def theirs(value, axis):
        return lax.dynamic_slice_in_dim(value, (1 - yh) * HC, HC, axis)

    def in_order(kept, got, axis):
        return jnp.concatenate([jnp.where(yh == 0, kept, got), jnp.where(yh == 0, got, kept)], axis=axis)

    channel = lax.rem(dp * PART + lax.broadcasted_iota(jnp.int32, (C, PART), 1), C)
    place = (channel == lax.broadcasted_iota(jnp.int32, (C, PART), 0)).astype(BF)
    slots = jnp.dot(place, conv_weight[0], preferred_element_type=F32).astype(BF)
    window = mine(slots, 0) + lax.ppermute(theirs(slots, 0), "yh", swap)
    x_in = section_inputs.reshape(POS, C)
    act = forward(x_in, norm_gain, norm_shift)
    window, act = lax.optimization_barrier((window, act))
    chunk = lax.all_to_all(
        jnp.broadcast_to(window[None], (NZ, HC, C)), "z", 0, 0, tiled=True
    ).reshape(SLOTS, C)
    fac = factors(
        flags, mine(x_in, 1), lax.ppermute(theirs(x_in, 1), "yh", swap),
        mine(norm_gain, 1), mine(norm_shift, 1),
    )

    top = top_grad.reshape(M, F, HW, C).transpose(1, 0, 2, 3).reshape(F, 1, M * HW, C)
    both = in_order(top, lax.ppermute(top, "yh", swap), 1).reshape(NYH * POS, C)
    arrived = (mine(both, 1), theirs(both, 1))
    act = act.reshape(F, 1, M * HW, C)
    act = in_order(act, lax.ppermute(act, "yh", swap), 1).reshape(NYH * POS, C)
    kernel_rows, (arrived, fac, act) = gather_x(
        chunk, lambda b: b[: SLOTS // 2], lambda b: b[SLOTS // 2 :], (arrived, fac, act)
    )
    pair_g = both
    pair_dx = None
    for k in range(4):
        if k > 0:
            pair_g = jnp.where(section == 3 - k, in_order(*arrived, 1), pair_g)
        sent = conv_back(3 - k, flags, arrived, s, kernel_rows, fac)
        if k == 0:
            sent, act = lax.optimization_barrier((sent, act))
            acts = gather_x(act, *clips_of_pair())
        pair_dx = sent if k == 0 else jnp.where(section == 3 - k, sent, pair_dx)
        if k < 3:
            src, dst = 3 - k, 2 - k
            same = lax.ppermute(sent, ("yl", "c"), [(src, dst)])
            cross = lax.ppermute(
                sent, ("yh", "yl", "c"), [(y * N_PIPE + src, (1 - y) * N_PIPE + dst) for y in range(NYH)]
            )
            arrived = (same, cross)

    pair_dx = pair_dx.reshape(F, NYH, M, HW, HC)
    kept = lax.dynamic_index_in_dim(pair_dx, yh, 1, False)
    given = lax.dynamic_index_in_dim(pair_dx, 1 - yh, 1, False)
    grads, (kept, given) = gather_x(pair_g, *clips_of_pair(), (kept, given))
    got = lax.ppermute(given, "yh", swap)
    dx = in_order(kept, got, -1).transpose(1, 0, 2, 3).reshape(section_inputs.shape)

    partial = weight_back(flags, acts[:3], grads[:3], wide_s)
    partial = weight_back(flags, acts[3:], grads[3:], wide_s, partial)
    weight_part = jnp.sum(lax.all_to_all(partial, "z", 0, 0, tiled=True).astype(F32), axis=0)
    return dx, weight_part[None]


def solution(mesh):
    fine = Mesh(mesh.devices.reshape(NX, NZ, NYH, 2, 2), ("x", "z", "yh", "yl", "c"))
    dp, pipe = ("x", "z", "yh"), ("yl", "c")
    placed = (
        P(pipe, dp, None, None, None, None, None),
        P(dp, None, None, None, None, None),
        P(pipe, None),
        P(pipe, None),
        P(pipe, dp, None),
    )
    return jax.shard_map(
        local,
        mesh=fine,
        in_specs=placed,
        out_specs=(P(pipe, dp, None, None, None, None, None), P(pipe, dp, None)),
        check_vma=False,
    )
```

```python
import functools

import jax
import jax.numpy as jnp
import numpy as np
from jax import lax
from jax.experimental import pallas as pl
from jax.experimental.pallas import tpu as pltpu
from jax.sharding import Mesh, PartitionSpec as P

C = 256
F = 4
H = 8
W = 4
M = 2
HW = H * W
POS = M * F * HW
ROWS = 27 * C
NX, NZ, NYH = 4, 8, 2
N_PIPE = 4
PART = ROWS // (NX * NZ * NYH)
PAIR = NYH * PART
CHUNK = NZ * PAIR
HC = C // NYH
SLOTS = NZ * HC
CLIPS = NX * NZ * NYH
GRANT = 24 << 20
BF = jnp.bfloat16
F32 = jnp.float32
HI = lax.Precision.HIGHEST
VMEM = pl.BlockSpec(memory_space=pltpu.VMEM)
SMEM = pl.BlockSpec(memory_space=pltpu.SMEM)
HBM = pl.BlockSpec(memory_space=pltpu.HBM)


def shift_matrices(size):
    s = np.zeros((9, size, size), np.float32)
    for kh in range(3):
        for kw in range(3):
            for h in range(H):
                for w in range(W):
                    h2, w2 = h - kh + 1, w - kw + 1
                    if 0 <= h2 < H and 0 <= w2 < W:
                        for f in range(size // HW):
                            s[kh * 3 + kw, f * HW + h * W + w, f * HW + h2 * W + w2] = 1
    return s


def group_matrix(channels):
    row = lax.div(lax.broadcasted_iota(jnp.int32, (channels, channels), 0), 8)
    column = lax.div(lax.broadcasted_iota(jnp.int32, (channels, channels), 1), 8)
    return jnp.where(row == column, 1.0 / (8 * HW), 0.0).astype(F32)


def spread(per_frame):
    frames, channels = per_frame.shape
    return jnp.broadcast_to(per_frame[:, None, :], (frames, HW, channels)).reshape(frames * HW, channels)


def frame_mean(value, group):
    sums = jnp.sum(value.reshape(-1, HW, value.shape[-1]), axis=1)
    return jnp.dot(sums, group, precision=HI, preferred_element_type=F32)


def time_major(m, t):
    return (t * M + m) * HW


def plain(m, t):
    return (m * F + t) * HW


def normalise(x, group):
    centred = x - spread(frame_mean(x, group))
    inv = lax.rsqrt(frame_mean(centred * centred, group) + 1e-06)
    return centred * spread(inv), inv


def forward_kernel(x_ref, gain_ref, shift_ref, act_ref, buf):
    for m in range(M):
        for t in range(F):
            buf[pl.ds(time_major(m, t), HW), :] = x_ref[pl.ds(plain(m, t), HW), :].astype(F32)
    xhat, _ = normalise(buf[...], group_matrix(C))
    normed = xhat * gain_ref[...] + shift_ref[...]
    act_ref[...] = (normed * jax.nn.sigmoid(normed)).astype(BF)


def forward(x, gain, shift):
    return pl.pallas_call(
        forward_kernel,
        out_shape=jax.ShapeDtypeStruct((POS, C), BF),
        in_specs=[VMEM] * 3,
        out_specs=VMEM,
        scratch_shapes=[pltpu.VMEM((POS, C), F32)],
        compiler_params=pltpu.CompilerParams(vmem_limit_bytes=GRANT),
        name="norm_forward",
    )(x, gain, shift)


def pair_row(k, m, t):
    return ((t * NYH + k) * M + m) * HW


def factors_kernel(flags, mine, theirs, gain_ref, shift_ref, out_ref, buf):
    first = flags[1] == 0
    for m in range(M):
        for t in range(F):
            a = mine[pl.ds(plain(m, t), HW), :].astype(F32)
            b = theirs[pl.ds(plain(m, t), HW), :].astype(F32)
            buf[pl.ds(pair_row(0, m, t), HW), :] = jnp.where(first, a, b)
            buf[pl.ds(pair_row(1, m, t), HW), :] = jnp.where(first, b, a)
    xhat, inv = normalise(buf[...], group_matrix(HC))
    gain = gain_ref[...]
    normed = xhat * gain + shift_ref[...]
    sig = jax.nn.sigmoid(normed)
    out_ref[0] = xhat
    out_ref[1] = sig * (1.0 + normed * (1.0 - sig)) * gain
    out_ref[2] = spread(inv)


def factors(flags, mine, theirs, gain, shift):
    return pl.pallas_call(
        factors_kernel,
        out_shape=jax.ShapeDtypeStruct((3, NYH * POS, HC), F32),
        in_specs=[SMEM] + [VMEM] * 4,
        out_specs=VMEM,
        scratch_shapes=[pltpu.VMEM((NYH * POS, HC), F32)],
        compiler_params=pltpu.CompilerParams(vmem_limit_bytes=GRANT),
        name="norm_factors",
    )(flags, mine, theirs, gain, shift)


def conv_kernel(target, flags, *refs):
    @pl.when(flags[2] == target)
    def _():
        conv_body(flags, *refs)


def conv_body(
    flags, cross, same, s_ref, own, left, right, far_a, far_b, fac,
    out_ref, kbuf, gs, krows,
):
    x = flags[0]
    yh = flags[1]
    rows = NYH * POS
    pieces = (
        (own, x * SLOTS, SLOTS),
        (left, lax.rem(x + NX - 1, NX) * SLOTS, SLOTS),
        (right, lax.rem(x + 1, NX) * SLOTS, SLOTS),
        (far_a, lax.rem(x + 2, NX) * SLOTS, SLOTS // 2),
        (far_b, lax.rem(x + 2, NX) * SLOTS + SLOTS // 2, SLOTS // 2),
    )
    for ref, at, size in pieces:
        kbuf[pl.ds(pl.multiple_of(at, HC), size), :] = ref[...]
    kept, got = same[...], cross[...]
    g = jnp.concatenate([jnp.where(yh == 0, kept, got), jnp.where(yh == 0, got, kept)], axis=1)
    for j in range(9):
        for r in range(rows // HC):
            gs[pl.ds(r * HC, HC), pl.ds(j * C, C)] = jnp.dot(
                s_ref[j], g[r * HC : (r + 1) * HC], preferred_element_type=F32
            ).astype(BF)
    slot = lax.broadcasted_iota(jnp.int32, (HC, C), 0)
    for kt in range(3):
        for j in range(9):
            row = (kt * 9 + j) * C + yh * HC
            window = lax.div(row, PAIR)
            after = jnp.minimum(window + 1, NX * NZ - 1)
            here = kbuf[pl.ds(pl.multiple_of(window * HC, HC), HC), :]
            there = kbuf[pl.ds(pl.multiple_of(after * HC, HC), HC), :]
            krows[pl.ds(kt * HC, HC), pl.ds(j * C, C)] = jnp.where(
                slot < (window + 1) * PAIR - row, here, there
            )
    product = lax.dot_general(
        gs[...], krows[...], (((1,), (1,)), ((), ())), preferred_element_type=F32
    )
    frame = rows // F
    grad_act = product[:, 2 * HC :]
    for kt in range(2):
        ahead = (2 - kt) * frame
        part = product[ahead:, kt * HC : (kt + 1) * HC]
        grad_act = grad_act + jnp.concatenate([part, jnp.zeros((ahead, HC), F32)], axis=0)
    xhat = fac[0]
    grad_hat = grad_act * fac[1]
    sums = jnp.concatenate(
        [jnp.sum(v.reshape(-1, HW, HC), axis=1) for v in (grad_hat, grad_hat * xhat)], axis=0
    )
    means = jnp.dot(sums, group_matrix(HC), precision=HI, preferred_element_type=F32)
    frames = rows // HW
    result = fac[2] * (grad_hat - spread(means[:frames]) - xhat * spread(means[frames:]))
    out_ref[...] = result.astype(BF)


def conv_back(target, flags, g, s, pieces, fac):
    rows = NYH * POS
    return pl.pallas_call(
        functools.partial(conv_kernel, target),
        out_shape=jax.ShapeDtypeStruct((rows, HC), BF),
        in_specs=[SMEM] + [VMEM] * 9,
        out_specs=VMEM,
        scratch_shapes=[
            pltpu.VMEM((NX * SLOTS, C), BF),
            pltpu.VMEM((rows, 9 * C), BF),
            pltpu.VMEM((3 * HC, 9 * C), BF),
        ],
        compiler_params=pltpu.CompilerParams(vmem_limit_bytes=GRANT),
        cost_estimate=pl.CostEstimate(flops=2 * POS * ROWS * C, bytes_accessed=ROWS * C, transcendentals=0),
        name="conv_back",
    )(flags, *g, s, *pieces, fac)


def weight_kernel(count, tail, *refs):
    flags, acts, grads, (s_ref, *before, out_ref) = (
        refs[0], refs[1 : 1 + count], refs[1 + count : 1 + 2 * count], refs[1 + 2 * count : -4 - count]
    )
    held, (turned, at, gbuf, sem) = refs[-4 - count : -4], refs[-4:]
    if tail:
        held, acts = acts, ()
    yh = flags[1]
    copies = [pltpu.make_async_copy(src, dst, sem.at[i]) for i, (src, dst) in enumerate(zip(acts, held))]
    for copy in copies:
        copy.start()
    wide = gbuf.shape[0] // F

    def frame(blocks, t):
        rows = blocks[0].shape[0] // F
        return jnp.concatenate([ref[pl.ds(t * rows, rows), :] for ref in blocks], axis=0)

    for t in range(F):
        gbuf[pl.ds(t * wide, wide), :] = frame(grads, t)
    turned[pl.ds(0, 2)] = jnp.zeros((2, C, wide), BF)
    for copy in copies:
        copy.wait()
    for t in range(F):
        turned[t + 2] = frame(held, t).astype(F32).T.astype(BF)
    first = lax.div(flags[0] * (CHUNK // 64), 4)
    for k in range(8):
        tap = jnp.minimum(first + k, 26)
        kt = lax.div(tap, 9)
        j = lax.rem(tap, 9)
        for t in range(F):
            for at_lane in range(0, wide, C):
                size = min(C, wide - at_lane)
                moved = s_ref[j, :size, :size]
                at[pl.ds(k * C, C), pl.ds(t * wide + at_lane, size)] = jnp.dot(
                    turned[t + kt, :, pl.ds(at_lane, size)], moved, preferred_element_type=F32
                ).astype(BF)
    offset = lax.rem(flags[0] * (CHUNK // 64), 4) * 64
    for z in range(NZ):
        skip = [(z * PAIR + k * PART) % 16 for k in range(NYH)]
        start = offset + jnp.where(yh == 0, z * PAIR - skip[0], z * PAIR + PART - skip[1])
        total = jnp.dot(
            at[pl.ds(pl.multiple_of(start, 16), HC), :], gbuf[...], preferred_element_type=F32
        )
        if before:
            total = total + before[0][z]
        if tail:
            total = total * (1.0 / CLIPS)
            total = jnp.where(yh == 0, total[skip[0] : skip[0] + PART], total[skip[1] : skip[1] + PART])
        out_ref[z] = total.astype(out_ref.dtype)


def weight_back(flags, acts, grads, s, before=None):
    tail = before is not None
    wide = sum(v.shape[0] // F for v in acts)
    return pl.pallas_call(
        functools.partial(weight_kernel, len(acts), tail),
        out_shape=jax.ShapeDtypeStruct((NZ, PART if tail else HC, C), BF if tail else F32),
        in_specs=[SMEM] + [VMEM if tail else HBM] * len(acts) + [VMEM] * len(grads) + [VMEM] * (1 + tail),
        out_specs=VMEM,
        scratch_shapes=[pltpu.VMEM(v.shape, BF) for v in acts]
        + [
            pltpu.VMEM((F + 2, C, wide), BF),
            pltpu.VMEM((8 * C, F * wide), BF),
            pltpu.VMEM((F * wide, C), BF),
            pltpu.SemaphoreType.DMA((len(acts),)),
        ],
        compiler_params=pltpu.CompilerParams(vmem_limit_bytes=GRANT),
        cost_estimate=pl.CostEstimate(
            flops=8 * CHUNK * wide * C, bytes_accessed=4 << 20, transcendentals=0
        ),
        name="weight_last" if tail else "weight_first",
    )(flags, *acts, *grads, s, *([before] if tail else []))


def ring(axis, step):
    n = lax.axis_size(axis)
    return [(i, (i + step) % n) for i in range(n)]


def gather_x(block, first_half, second_half, between=None):
    left = lax.ppermute(block, "x", ring("x", 1))
    right = lax.ppermute(block, "x", ring("x", -1))
    if between is not None:
        left, right, between = lax.optimization_barrier((left, right, between))
    far_a = lax.ppermute(first_half(left), "x", ring("x", 1))
    far_b = lax.ppermute(second_half(right), "x", ring("x", -1))
    blocks = (block, left, right, far_a, far_b)
    return blocks if between is None else (blocks, between)


def clips_of_pair():
    def pick(k):
        return lambda b: b.reshape(F, NYH, M * HW, C)[:, k].reshape(POS, C)

    return pick(0), pick(1)


def local(section_inputs, top_grad, norm_gain, norm_shift, conv_weight):
    s = jnp.asarray(shift_matrices(HC), BF)
    wide_s = jnp.asarray(shift_matrices(C), BF)
    x_at = lax.axis_index("x")
    yh = lax.axis_index("yh")
    dp = (x_at * NZ + lax.axis_index("z")) * NYH + yh
    section = lax.axis_index("yl") * 2 + lax.axis_index("c")
    flags = jnp.stack([x_at, yh, section]).astype(jnp.int32)
    swap = ring("yh", 1)

    def mine(value, axis):
        return lax.dynamic_slice_in_dim(value, yh * HC, HC, axis)

    def theirs(value, axis):
        return lax.dynamic_slice_in_dim(value, (1 - yh) * HC, HC, axis)

    def in_order(kept, got, axis):
        return jnp.concatenate([jnp.where(yh == 0, kept, got), jnp.where(yh == 0, got, kept)], axis=axis)

    channel = lax.rem(dp * PART + lax.broadcasted_iota(jnp.int32, (C, PART), 1), C)
    place = (channel == lax.broadcasted_iota(jnp.int32, (C, PART), 0)).astype(BF)
    slots = jnp.dot(place, conv_weight[0], preferred_element_type=F32).astype(BF)
    other = lax.ppermute(theirs(slots, 0), "yh", swap)
    x_in = section_inputs.reshape(POS, C)
    act = forward(x_in, norm_gain, norm_shift)
    other, act = lax.optimization_barrier((other, act))
    window = mine(slots, 0) + other
    chunk = lax.all_to_all(
        jnp.broadcast_to(window[None], (NZ, HC, C)), "z", 0, 0, tiled=True
    ).reshape(SLOTS, C)
    fac = factors(
        flags, mine(x_in, 1), lax.ppermute(theirs(x_in, 1), "yh", swap),
        mine(norm_gain, 1), mine(norm_shift, 1),
    )

    top = top_grad.reshape(M, F, HW, C).transpose(1, 0, 2, 3).reshape(F, 1, M * HW, C)
    both = in_order(top, lax.ppermute(top, "yh", swap), 1).reshape(NYH * POS, C)
    arrived = (mine(both, 1), theirs(both, 1))
    act = act.reshape(F, 1, M * HW, C)
    act = in_order(act, lax.ppermute(act, "yh", swap), 1).reshape(NYH * POS, C)
    kernel_rows, (arrived, fac, act) = gather_x(
        chunk, lambda b: b[: SLOTS // 2], lambda b: b[SLOTS // 2 :], (arrived, fac, act)
    )
    pair_g = both
    pair_dx = None
    for k in range(4):
        if k > 0:
            same, cross = arrived
            both = [jnp.where(yh == 1, cross, same), jnp.where(yh == 1, same, cross)]
            pair_g = jnp.where(section == 3 - k, jnp.concatenate(both, axis=1), pair_g)
        sent = conv_back(3 - k, flags, arrived[::-1], s, kernel_rows, fac)
        if k == 0:
            sent, act = lax.optimization_barrier((sent, act))
            acts = gather_x(act, *clips_of_pair())
        pair_dx = sent if k == 0 else jnp.where(section == 3 - k, sent, pair_dx)
        if k < 3:
            src, dst = 3 - k, 2 - k
            same = lax.ppermute(sent, ("yl", "c"), [(src, dst)])
            cross = lax.ppermute(
                sent, ("yh", "yl", "c"), [(y * N_PIPE + src, (1 - y) * N_PIPE + dst) for y in range(NYH)]
            )
            arrived = (same, cross)

    pair_dx = pair_dx.reshape(F, NYH, M, HW, HC)
    kept = lax.dynamic_index_in_dim(pair_dx, yh, 1, False)
    given = lax.dynamic_index_in_dim(pair_dx, 1 - yh, 1, False)
    grads, (kept, given) = gather_x(pair_g, *clips_of_pair(), (kept, given))
    got = lax.ppermute(given, "yh", swap)
    dx = in_order(kept, got, -1).transpose(1, 0, 2, 3).reshape(section_inputs.shape)

    partial = weight_back(flags, acts[:3], grads[:3], wide_s)
    partial = weight_back(flags, acts[3:], grads[3:], wide_s, partial)
    parts = lax.all_to_all(partial, "z", 0, 0, tiled=True).reshape(NZ, 1, PART, C)
    return dx, jnp.sum(parts.astype(F32), axis=0)


def solution(mesh):
    fine = Mesh(mesh.devices.reshape(NX, NZ, NYH, 2, 2), ("x", "z", "yh", "yl", "c"))
    dp, pipe = ("x", "z", "yh"), ("yl", "c")
    placed = (
        P(pipe, dp, None, None, None, None, None),
        P(dp, None, None, None, None, None),
        P(pipe, None),
        P(pipe, None),
        P(pipe, dp, None),
    )
    return jax.shard_map(
        local,
        mesh=fine,
        in_specs=placed,
        out_specs=(P(pipe, dp, None, None, None, None, None), P(pipe, dp, None)),
        check_vma=False,
    )
```

```python
import functools

import jax
import jax.numpy as jnp
import numpy as np
from jax import lax
from jax.experimental import pallas as pl
from jax.experimental.pallas import tpu as pltpu
from jax.sharding import Mesh, PartitionSpec as P

C = 256
F = 4
H = 8
W = 4
M = 2
HW = H * W
POS = M * F * HW
ROWS = 27 * C
NX, NZ, NYH = 4, 8, 2
N_PIPE = 4
PART = ROWS // (NX * NZ * NYH)
PAIR = NYH * PART
CHUNK = NZ * PAIR
HC = C // NYH
SLOTS = NZ * HC
CLIPS = NX * NZ * NYH
GRANT = 24 << 20
BF = jnp.bfloat16
F32 = jnp.float32
HI = lax.Precision.HIGHEST
VMEM = pl.BlockSpec(memory_space=pltpu.VMEM)
SMEM = pl.BlockSpec(memory_space=pltpu.SMEM)
HBM = pl.BlockSpec(memory_space=pltpu.HBM)


def shift_matrices(size):
    s = np.zeros((9, size, size), np.float32)
    for kh in range(3):
        for kw in range(3):
            for h in range(H):
                for w in range(W):
                    h2, w2 = h - kh + 1, w - kw + 1
                    if 0 <= h2 < H and 0 <= w2 < W:
                        for f in range(size // HW):
                            s[kh * 3 + kw, f * HW + h * W + w, f * HW + h2 * W + w2] = 1
    return s


def group_matrix(channels):
    row = lax.div(lax.broadcasted_iota(jnp.int32, (channels, channels), 0), 8)
    column = lax.div(lax.broadcasted_iota(jnp.int32, (channels, channels), 1), 8)
    return jnp.where(row == column, 1.0 / (8 * HW), 0.0).astype(F32)


def spread(per_frame):
    frames, channels = per_frame.shape
    return jnp.broadcast_to(per_frame[:, None, :], (frames, HW, channels)).reshape(frames * HW, channels)


def frame_mean(value, group):
    sums = jnp.sum(value.reshape(-1, HW, value.shape[-1]), axis=1)
    return jnp.dot(sums, group, precision=HI, preferred_element_type=F32)


def time_major(m, t):
    return (t * M + m) * HW


def plain(m, t):
    return (m * F + t) * HW


def normalise(x, group):
    centred = x - spread(frame_mean(x, group))
    inv = lax.rsqrt(frame_mean(centred * centred, group) + 1e-06)
    return centred * spread(inv), inv


def forward_kernel(x_ref, gain_ref, shift_ref, act_ref, buf):
    for m in range(M):
        for t in range(F):
            buf[pl.ds(time_major(m, t), HW), :] = x_ref[pl.ds(plain(m, t), HW), :].astype(F32)
    xhat, _ = normalise(buf[...], group_matrix(C))
    normed = xhat * gain_ref[...] + shift_ref[...]
    act_ref[...] = (normed * jax.nn.sigmoid(normed)).astype(BF)


def forward(x, gain, shift):
    return pl.pallas_call(
        forward_kernel,
        out_shape=jax.ShapeDtypeStruct((POS, C), BF),
        in_specs=[VMEM] * 3,
        out_specs=VMEM,
        scratch_shapes=[pltpu.VMEM((POS, C), F32)],
        compiler_params=pltpu.CompilerParams(vmem_limit_bytes=GRANT),
        name="norm_forward",
    )(x, gain, shift)


def pair_row(k, m, t):
    return ((t * NYH + k) * M + m) * HW


def factors_kernel(flags, mine, theirs, gain_ref, shift_ref, out_ref, buf):
    first = flags[1] == 0
    for m in range(M):
        for t in range(F):
            a = mine[pl.ds(plain(m, t), HW), :].astype(F32)
            b = theirs[pl.ds(plain(m, t), HW), :].astype(F32)
            buf[pl.ds(pair_row(0, m, t), HW), :] = jnp.where(first, a, b)
            buf[pl.ds(pair_row(1, m, t), HW), :] = jnp.where(first, b, a)
    xhat, inv = normalise(buf[...], group_matrix(HC))
    gain = gain_ref[...]
    normed = xhat * gain + shift_ref[...]
    sig = jax.nn.sigmoid(normed)
    out_ref[0] = xhat
    out_ref[1] = sig * (1.0 + normed * (1.0 - sig)) * gain
    out_ref[2] = spread(inv)


def factors(flags, mine, theirs, gain, shift):
    return pl.pallas_call(
        factors_kernel,
        out_shape=jax.ShapeDtypeStruct((3, NYH * POS, HC), F32),
        in_specs=[SMEM] + [VMEM] * 4,
        out_specs=VMEM,
        scratch_shapes=[pltpu.VMEM((NYH * POS, HC), F32)],
        compiler_params=pltpu.CompilerParams(vmem_limit_bytes=GRANT),
        name="norm_factors",
    )(flags, mine, theirs, gain, shift)


def conv_kernel(target, flags, *refs):
    @pl.when((flags[2] == target) | (target == 0))
    def _():
        conv_body(flags, *refs)


def conv_body(
    flags, cross, same, s_ref, own, left, right, far_a, far_b, fac,
    out_ref, kbuf, gs, krows,
):
    x = flags[0]
    yh = flags[1]
    rows = NYH * POS
    pieces = (
        (own, x * SLOTS, SLOTS),
        (left, lax.rem(x + NX - 1, NX) * SLOTS, SLOTS),
        (right, lax.rem(x + 1, NX) * SLOTS, SLOTS),
        (far_a, lax.rem(x + 2, NX) * SLOTS, SLOTS // 2),
        (far_b, lax.rem(x + 2, NX) * SLOTS + SLOTS // 2, SLOTS // 2),
    )
    for ref, at, size in pieces:
        kbuf[pl.ds(pl.multiple_of(at, HC), size), :] = ref[...]
    kept, got = same[...], cross[...]
    g = jnp.concatenate([jnp.where(yh == 0, kept, got), jnp.where(yh == 0, got, kept)], axis=1)
    for j in range(9):
        for r in range(rows // HC):
            gs[pl.ds(r * HC, HC), pl.ds(j * C, C)] = jnp.dot(
                s_ref[j], g[r * HC : (r + 1) * HC], preferred_element_type=F32
            ).astype(BF)
    slot = lax.broadcasted_iota(jnp.int32, (HC, C), 0)
    for kt in range(3):
        for j in range(9):
            row = (kt * 9 + j) * C + yh * HC
            window = lax.div(row, PAIR)
            after = jnp.minimum(window + 1, NX * NZ - 1)
            here = kbuf[pl.ds(pl.multiple_of(window * HC, HC), HC), :]
            there = kbuf[pl.ds(pl.multiple_of(after * HC, HC), HC), :]
            krows[pl.ds(kt * HC, HC), pl.ds(j * C, C)] = jnp.where(
                slot < (window + 1) * PAIR - row, here, there
            )
    product = lax.dot_general(
        gs[...], krows[...], (((1,), (1,)), ((), ())), preferred_element_type=F32
    )
    frame = rows // F
    grad_act = product[:, 2 * HC :]
    for kt in range(2):
        ahead = (2 - kt) * frame
        part = product[ahead:, kt * HC : (kt + 1) * HC]
        grad_act = grad_act + jnp.concatenate([part, jnp.zeros((ahead, HC), F32)], axis=0)
    xhat = fac[0]
    grad_hat = grad_act * fac[1]
    sums = jnp.concatenate(
        [jnp.sum(v.reshape(-1, HW, HC), axis=1) for v in (grad_hat, grad_hat * xhat)], axis=0
    )
    means = jnp.dot(sums, group_matrix(HC), precision=HI, preferred_element_type=F32)
    frames = rows // HW
    result = fac[2] * (grad_hat - spread(means[:frames]) - xhat * spread(means[frames:]))
    out_ref[...] = result.astype(BF)


def conv_back(target, flags, g, s, pieces, fac):
    rows = NYH * POS
    return pl.pallas_call(
        functools.partial(conv_kernel, target),
        out_shape=jax.ShapeDtypeStruct((rows, HC), BF),
        in_specs=[SMEM] + [VMEM] * 9,
        out_specs=VMEM,
        scratch_shapes=[
            pltpu.VMEM((NX * SLOTS, C), BF),
            pltpu.VMEM((rows, 9 * C), BF),
            pltpu.VMEM((3 * HC, 9 * C), BF),
        ],
        compiler_params=pltpu.CompilerParams(vmem_limit_bytes=GRANT),
        cost_estimate=pl.CostEstimate(flops=2 * POS * ROWS * C, bytes_accessed=ROWS * C, transcendentals=0),
        name="conv_back",
    )(flags, *g, s, *pieces, fac)


def weight_kernel(count, tail, *refs):
    flags, acts, grads, (s_ref, *before, out_ref) = (
        refs[0], refs[1 : 1 + count], refs[1 + count : 1 + 2 * count], refs[1 + 2 * count : -4 - count]
    )
    held, (turned, at, gbuf, sem) = refs[-4 - count : -4], refs[-4:]
    if tail:
        held, acts = acts, ()
    yh = flags[1]
    copies = [pltpu.make_async_copy(src, dst, sem.at[i]) for i, (src, dst) in enumerate(zip(acts, held))]
    for copy in copies:
        copy.start()
    wide = gbuf.shape[0] // F

    def frame(blocks, t):
        rows = blocks[0].shape[0] // F
        return jnp.concatenate([ref[pl.ds(t * rows, rows), :] for ref in blocks], axis=0)

    for t in range(F):
        gbuf[pl.ds(t * wide, wide), :] = frame(grads, t)
    turned[pl.ds(0, 2)] = jnp.zeros((2, C, wide), BF)
    for copy in copies:
        copy.wait()
    for t in range(F):
        turned[t + 2] = frame(held, t).astype(F32).T.astype(BF)
    first = lax.div(flags[0] * (CHUNK // 64), 4)
    for k in range(8):
        tap = jnp.minimum(first + k, 26)
        kt = lax.div(tap, 9)
        j = lax.rem(tap, 9)
        for t in range(F):
            for at_lane in range(0, wide, C):
                size = min(C, wide - at_lane)
                moved = s_ref[j, :size, :size]
                at[pl.ds(k * C, C), pl.ds(t * wide + at_lane, size)] = jnp.dot(
                    turned[t + kt, :, pl.ds(at_lane, size)], moved, preferred_element_type=F32
                ).astype(BF)
    offset = lax.rem(flags[0] * (CHUNK // 64), 4) * 64
    for z in range(NZ):
        skip = [(z * PAIR + k * PART) % 16 for k in range(NYH)]
        start = offset + jnp.where(yh == 0, z * PAIR - skip[0], z * PAIR + PART - skip[1])
        total = jnp.dot(
            at[pl.ds(pl.multiple_of(start, 16), HC), :], gbuf[...], preferred_element_type=F32
        )
        if before:
            total = total + before[0][z]
        if tail:
            total = total * (1.0 / CLIPS)
            total = jnp.where(yh == 0, total[skip[0] : skip[0] + PART], total[skip[1] : skip[1] + PART])
        out_ref[z] = total.astype(out_ref.dtype)


def weight_back(flags, acts, grads, s, before=None):
    tail = before is not None
    wide = sum(v.shape[0] // F for v in acts)
    return pl.pallas_call(
        functools.partial(weight_kernel, len(acts), tail),
        out_shape=jax.ShapeDtypeStruct((NZ, PART if tail else HC, C), BF if tail else F32),
        in_specs=[SMEM] + [VMEM if tail else HBM] * len(acts) + [VMEM] * len(grads) + [VMEM] * (1 + tail),
        out_specs=VMEM,
        scratch_shapes=[pltpu.VMEM(v.shape, BF) for v in acts]
        + [
            pltpu.VMEM((F + 2, C, wide), BF),
            pltpu.VMEM((8 * C, F * wide), BF),
            pltpu.VMEM((F * wide, C), BF),
            pltpu.SemaphoreType.DMA((len(acts),)),
        ],
        compiler_params=pltpu.CompilerParams(vmem_limit_bytes=GRANT),
        cost_estimate=pl.CostEstimate(
            flops=8 * CHUNK * wide * C, bytes_accessed=4 << 20, transcendentals=0
        ),
        name="weight_last" if tail else "weight_first",
    )(flags, *acts, *grads, s, *([before] if tail else []))


def ring(axis, step):
    n = lax.axis_size(axis)
    return [(i, (i + step) % n) for i in range(n)]


def gather_x(block, first_half, second_half, between=None):
    left = lax.ppermute(block, "x", ring("x", 1))
    right = lax.ppermute(block, "x", ring("x", -1))
    if between is not None:
        left, between = lax.optimization_barrier((left, between))
    far_a = lax.ppermute(first_half(left), "x", ring("x", 1))
    far_b = lax.ppermute(second_half(right), "x", ring("x", -1))
    blocks = (block, left, right, far_a, far_b)
    return blocks if between is None else (blocks, between)


def clips_of_pair():
    def pick(k):
        return lambda b: b.reshape(F, NYH, M * HW, C)[:, k].reshape(POS, C)

    return pick(0), pick(1)


def local(section_inputs, top_grad, norm_gain, norm_shift, conv_weight):
    s = jnp.asarray(shift_matrices(HC), BF)
    wide_s = jnp.asarray(shift_matrices(C), BF)
    x_at = lax.axis_index("x")
    yh = lax.axis_index("yh")
    dp = (x_at * NZ + lax.axis_index("z")) * NYH + yh
    section = lax.axis_index("yl") * 2 + lax.axis_index("c")
    flags = jnp.stack([x_at, yh, section]).astype(jnp.int32)
    swap = ring("yh", 1)

    def mine(value, axis):
        return lax.dynamic_slice_in_dim(value, yh * HC, HC, axis)

    def theirs(value, axis):
        return lax.dynamic_slice_in_dim(value, (1 - yh) * HC, HC, axis)

    def in_order(kept, got, axis):
        return jnp.concatenate([jnp.where(yh == 0, kept, got), jnp.where(yh == 0, got, kept)], axis=axis)

    channel = lax.rem(dp * PART + lax.broadcasted_iota(jnp.int32, (C, PART), 1), C)
    place = (channel == lax.broadcasted_iota(jnp.int32, (C, PART), 0)).astype(BF)
    slots = jnp.dot(place, conv_weight[0], preferred_element_type=F32).astype(BF)
    other = lax.ppermute(theirs(slots, 0), "yh", swap)
    x_in = section_inputs.reshape(POS, C)
    act = forward(x_in, norm_gain, norm_shift)
    other, act = lax.optimization_barrier((other, act))
    window = mine(slots, 0) + other
    chunk = lax.all_to_all(
        jnp.broadcast_to(window[None], (NZ, HC, C)), "z", 0, 0, tiled=True
    ).reshape(SLOTS, C)
    fac = factors(
        flags, mine(x_in, 1), lax.ppermute(theirs(x_in, 1), "yh", swap),
        mine(norm_gain, 1), mine(norm_shift, 1),
    )

    top = top_grad.reshape(M, F, HW, C).transpose(1, 0, 2, 3).reshape(F, 1, M * HW, C)
    both = in_order(top, lax.ppermute(top, "yh", swap), 1).reshape(NYH * POS, C)
    arrived = (mine(both, 1), theirs(both, 1))
    act = act.reshape(F, 1, M * HW, C)
    act = in_order(act, lax.ppermute(act, "yh", swap), 1).reshape(NYH * POS, C)
    kernel_rows, (arrived, fac, act) = gather_x(
        chunk, lambda b: b[: SLOTS // 2], lambda b: b[SLOTS // 2 :], (arrived, fac, act)
    )
    pair_g = both
    for k in range(4):
        if k > 0:
            same, cross = arrived
            both = [jnp.where(yh == 1, cross, same), jnp.where(yh == 1, same, cross)]
            pair_g = jnp.where(section == 3 - k, jnp.concatenate(both, axis=1), pair_g)
        if k == 3:
            arrived = (mine(pair_g, 1), theirs(pair_g, 1))
        sent = conv_back(3 - k, flags, arrived[::-1], s, kernel_rows, fac)
        if k == 0:
            sent, act = lax.optimization_barrier((sent, act))
            acts = gather_x(act, *clips_of_pair())
        if k < 3:
            src, dst = 3 - k, 2 - k
            same = lax.ppermute(sent, ("yl", "c"), [(src, dst)])
            cross = lax.ppermute(
                sent, ("yh", "yl", "c"), [(y * N_PIPE + src, (1 - y) * N_PIPE + dst) for y in range(NYH)]
            )
            arrived = (same, cross)

    pair_dx = sent.reshape(F, NYH, M, HW, HC)
    kept = lax.dynamic_index_in_dim(pair_dx, yh, 1, False)
    given = lax.dynamic_index_in_dim(pair_dx, 1 - yh, 1, False)
    grads, (kept, given) = gather_x(pair_g, *clips_of_pair(), (kept, given))
    got = lax.ppermute(given, "yh", swap)
    dx = in_order(kept, got, -1).transpose(1, 0, 2, 3).reshape(section_inputs.shape)

    partial = weight_back(flags, acts[:3], grads[:3], wide_s)
    partial = weight_back(flags, acts[3:], grads[3:], wide_s, partial)
    parts = lax.all_to_all(partial, "z", 0, 0, tiled=True).reshape(NZ, 1, PART, C)
    return dx, jnp.sum(parts.astype(F32), axis=0)


def solution(mesh):
    fine = Mesh(mesh.devices.reshape(NX, NZ, NYH, 2, 2), ("x", "z", "yh", "yl", "c"))
    dp, pipe = ("x", "z", "yh"), ("yl", "c")
    placed = (
        P(pipe, dp, None, None, None, None, None),
        P(dp, None, None, None, None, None),
        P(pipe, None),
        P(pipe, None),
        P(pipe, dp, None),
    )
    return jax.shard_map(
        local,
        mesh=fine,
        in_specs=placed,
        out_specs=(P(pipe, dp, None, None, None, None, None), P(pipe, dp, None)),
        check_vma=False,
    )
```

```python
import functools

import jax
import jax.numpy as jnp
import numpy as np
from jax import lax
from jax.experimental import pallas as pl
from jax.experimental.pallas import tpu as pltpu
from jax.sharding import Mesh, PartitionSpec as P

C = 256
F = 4
H = 8
W = 4
M = 2
HW = H * W
POS = M * F * HW
ROWS = 27 * C
NX, NZ, NYH = 4, 8, 2
N_PIPE = 4
PART = ROWS // (NX * NZ * NYH)
PAIR = NYH * PART
CHUNK = NZ * PAIR
HC = C // NYH
SLOTS = NZ * HC
CLIPS = NX * NZ * NYH
GRANT = 24 << 20
BF = jnp.bfloat16
F32 = jnp.float32
HI = lax.Precision.HIGHEST
VMEM = pl.BlockSpec(memory_space=pltpu.VMEM)
SMEM = pl.BlockSpec(memory_space=pltpu.SMEM)
HBM = pl.BlockSpec(memory_space=pltpu.HBM)


def shift_matrices(size):
    s = np.zeros((9, size, size), np.float32)
    for kh in range(3):
        for kw in range(3):
            for h in range(H):
                for w in range(W):
                    h2, w2 = h - kh + 1, w - kw + 1
                    if 0 <= h2 < H and 0 <= w2 < W:
                        for f in range(size // HW):
                            s[kh * 3 + kw, f * HW + h * W + w, f * HW + h2 * W + w2] = 1
    return s


def group_matrix(channels):
    row = lax.div(lax.broadcasted_iota(jnp.int32, (channels, channels), 0), 8)
    column = lax.div(lax.broadcasted_iota(jnp.int32, (channels, channels), 1), 8)
    return jnp.where(row == column, 1.0 / (8 * HW), 0.0).astype(F32)


def spread(per_frame):
    frames, channels = per_frame.shape
    return jnp.broadcast_to(per_frame[:, None, :], (frames, HW, channels)).reshape(frames * HW, channels)


def frame_mean(value, group):
    sums = jnp.sum(value.reshape(-1, HW, value.shape[-1]), axis=1)
    return jnp.dot(sums, group, precision=HI, preferred_element_type=F32)


def time_major(m, t):
    return (t * M + m) * HW


def plain(m, t):
    return (m * F + t) * HW


def normalise(x, group):
    centred = x - spread(frame_mean(x, group))
    inv = lax.rsqrt(frame_mean(centred * centred, group) + 1e-06)
    return centred * spread(inv), inv


def forward_kernel(x_ref, gain_ref, shift_ref, act_ref, buf):
    for m in range(M):
        for t in range(F):
            buf[pl.ds(time_major(m, t), HW), :] = x_ref[pl.ds(plain(m, t), HW), :].astype(F32)
    xhat, _ = normalise(buf[...], group_matrix(C))
    normed = xhat * gain_ref[...] + shift_ref[...]
    act_ref[...] = (normed * jax.nn.sigmoid(normed)).astype(BF)


def forward(x, gain, shift):
    return pl.pallas_call(
        forward_kernel,
        out_shape=jax.ShapeDtypeStruct((POS, C), BF),
        in_specs=[VMEM] * 3,
        out_specs=VMEM,
        scratch_shapes=[pltpu.VMEM((POS, C), F32)],
        compiler_params=pltpu.CompilerParams(vmem_limit_bytes=GRANT),
        name="norm_forward",
    )(x, gain, shift)


def pair_row(k, m, t):
    return ((t * NYH + k) * M + m) * HW


def factors_kernel(flags, mine, theirs, gain_ref, shift_ref, out_ref, buf):
    first = flags[1] == 0
    for m in range(M):
        for t in range(F):
            a = mine[pl.ds(plain(m, t), HW), :].astype(F32)
            b = theirs[pl.ds(plain(m, t), HW), :].astype(F32)
            buf[pl.ds(pair_row(0, m, t), HW), :] = jnp.where(first, a, b)
            buf[pl.ds(pair_row(1, m, t), HW), :] = jnp.where(first, b, a)
    xhat, inv = normalise(buf[...], group_matrix(HC))
    gain = gain_ref[...]
    normed = xhat * gain + shift_ref[...]
    sig = jax.nn.sigmoid(normed)
    out_ref[0] = xhat
    out_ref[1] = sig * (1.0 + normed * (1.0 - sig)) * gain
    out_ref[2] = spread(inv)


def factors(flags, mine, theirs, gain, shift):
    return pl.pallas_call(
        factors_kernel,
        out_shape=jax.ShapeDtypeStruct((3, NYH * POS, HC), F32),
        in_specs=[SMEM] + [VMEM] * 4,
        out_specs=VMEM,
        scratch_shapes=[pltpu.VMEM((NYH * POS, HC), F32)],
        compiler_params=pltpu.CompilerParams(vmem_limit_bytes=GRANT),
        name="norm_factors",
    )(flags, mine, theirs, gain, shift)


def conv_kernel(target, flags, *refs):
    @pl.when((flags[2] == target) | (target == 0))
    def _():
        conv_body(flags, *refs)


def conv_body(
    flags, cross, same, s_ref, own, left, right, far_a, far_b, fac,
    out_ref, kbuf, gs, krows,
):
    x = flags[0]
    yh = flags[1]
    rows = NYH * POS
    pieces = (
        (own, x * SLOTS, SLOTS),
        (left, lax.rem(x + NX - 1, NX) * SLOTS, SLOTS),
        (right, lax.rem(x + 1, NX) * SLOTS, SLOTS),
        (far_a, lax.rem(x + 2, NX) * SLOTS, SLOTS // 2),
        (far_b, lax.rem(x + 2, NX) * SLOTS + SLOTS // 2, SLOTS // 2),
    )
    for ref, at, size in pieces:
        kbuf[pl.ds(pl.multiple_of(at, HC), size), :] = ref[...]
    kept, got = same[...], cross[...]
    g = jnp.concatenate([jnp.where(yh == 0, kept, got), jnp.where(yh == 0, got, kept)], axis=1)
    for j in range(9):
        for r in range(rows // HC):
            gs[pl.ds(r * HC, HC), pl.ds(j * C, C)] = jnp.dot(
                s_ref[j], g[r * HC : (r + 1) * HC], preferred_element_type=F32
            ).astype(BF)
    slot = lax.broadcasted_iota(jnp.int32, (HC, C), 0)
    for kt in range(3):
        for j in range(9):
            row = (kt * 9 + j) * C + yh * HC
            window = lax.div(row, PAIR)
            after = jnp.minimum(window + 1, NX * NZ - 1)
            here = kbuf[pl.ds(pl.multiple_of(window * HC, HC), HC), :]
            there = kbuf[pl.ds(pl.multiple_of(after * HC, HC), HC), :]
            krows[pl.ds(kt * HC, HC), pl.ds(j * C, C)] = jnp.where(
                slot < (window + 1) * PAIR - row, here, there
            )
    product = lax.dot_general(
        gs[...], krows[...], (((1,), (1,)), ((), ())), preferred_element_type=F32
    )
    frame = rows // F
    grad_act = product[:, 2 * HC :]
    for kt in range(2):
        ahead = (2 - kt) * frame
        part = product[ahead:, kt * HC : (kt + 1) * HC]
        grad_act = grad_act + jnp.concatenate([part, jnp.zeros((ahead, HC), F32)], axis=0)
    xhat = fac[0]
    grad_hat = grad_act * fac[1]
    sums = jnp.concatenate(
        [jnp.sum(v.reshape(-1, HW, HC), axis=1) for v in (grad_hat, grad_hat * xhat)], axis=0
    )
    means = jnp.dot(sums, group_matrix(HC), precision=HI, preferred_element_type=F32)
    frames = rows // HW
    result = fac[2] * (grad_hat - spread(means[:frames]) - xhat * spread(means[frames:]))
    out_ref[...] = result.astype(BF)


def conv_back(target, flags, g, s, pieces, fac):
    rows = NYH * POS
    return pl.pallas_call(
        functools.partial(conv_kernel, target),
        out_shape=jax.ShapeDtypeStruct((rows, HC), BF),
        in_specs=[SMEM] + [VMEM] * 9,
        out_specs=VMEM,
        scratch_shapes=[
            pltpu.VMEM((NX * SLOTS, C), BF),
            pltpu.VMEM((rows, 9 * C), BF),
            pltpu.VMEM((3 * HC, 9 * C), BF),
        ],
        compiler_params=pltpu.CompilerParams(vmem_limit_bytes=GRANT),
        cost_estimate=pl.CostEstimate(flops=2 * POS * ROWS * C, bytes_accessed=ROWS * C, transcendentals=0),
        name="conv_back",
    )(flags, *g, s, *pieces, fac)


def weight_kernel(count, tail, *refs):
    flags, acts, grads, (s_ref, *before, out_ref) = (
        refs[0], refs[1 : 1 + count], refs[1 + count : 1 + 2 * count], refs[1 + 2 * count : -4 - count]
    )
    held, (turned, at, gbuf, sem) = refs[-4 - count : -4], refs[-4:]
    if tail:
        held, acts = acts, ()
    yh = flags[1]
    copies = [pltpu.make_async_copy(src, dst, sem.at[i]) for i, (src, dst) in enumerate(zip(acts, held))]
    for copy in copies:
        copy.start()
    wide = gbuf.shape[0] // F

    def frame(blocks, t):
        rows = blocks[0].shape[0] // F
        return jnp.concatenate([ref[pl.ds(t * rows, rows), :] for ref in blocks], axis=0)

    for t in range(F):
        gbuf[pl.ds(t * wide, wide), :] = frame(grads, t)
    turned[pl.ds(0, 2)] = jnp.zeros((2, C, wide), BF)
    for copy in copies:
        copy.wait()
    for t in range(F):
        turned[t + 2] = frame(held, t).astype(F32).T.astype(BF)
    first = lax.div(flags[0] * (CHUNK // 64), 4)
    for k in range(8):
        tap = jnp.minimum(first + k, 26)
        kt = lax.div(tap, 9)
        j = lax.rem(tap, 9)
        for t in range(F):
            for at_lane in range(0, wide, C):
                size = min(C, wide - at_lane)
                moved = s_ref[j, :size, :size]
                at[pl.ds(k * C, C), pl.ds(t * wide + at_lane, size)] = jnp.dot(
                    turned[t + kt, :, pl.ds(at_lane, size)], moved, preferred_element_type=F32
                ).astype(BF)
    offset = lax.rem(flags[0] * (CHUNK // 64), 4) * 64
    for z in range(NZ):
        skip = [(z * PAIR + k * PART) % 16 for k in range(NYH)]
        start = offset + jnp.where(yh == 0, z * PAIR - skip[0], z * PAIR + PART - skip[1])
        total = jnp.dot(
            at[pl.ds(pl.multiple_of(start, 16), HC), :], gbuf[...], preferred_element_type=F32
        )
        if before:
            total = total + before[0][z]
        if tail:
            total = total * (1.0 / CLIPS)
            total = jnp.where(yh == 0, total[skip[0] : skip[0] + PART], total[skip[1] : skip[1] + PART])
        out_ref[z] = total.astype(out_ref.dtype)


def weight_back(flags, acts, grads, s, before=None):
    tail = before is not None
    wide = sum(v.shape[0] // F for v in acts)
    return pl.pallas_call(
        functools.partial(weight_kernel, len(acts), tail),
        out_shape=jax.ShapeDtypeStruct((NZ, PART if tail else HC, C), BF if tail else F32),
        in_specs=[SMEM] + [VMEM if tail else HBM] * len(acts) + [VMEM] * len(grads) + [VMEM] * (1 + tail),
        out_specs=VMEM,
        scratch_shapes=[pltpu.VMEM(v.shape, BF) for v in acts]
        + [
            pltpu.VMEM((F + 2, C, wide), BF),
            pltpu.VMEM((8 * C, F * wide), BF),
            pltpu.VMEM((F * wide, C), BF),
            pltpu.SemaphoreType.DMA((len(acts),)),
        ],
        compiler_params=pltpu.CompilerParams(vmem_limit_bytes=GRANT),
        cost_estimate=pl.CostEstimate(
            flops=8 * CHUNK * wide * C, bytes_accessed=4 << 20, transcendentals=0
        ),
        name="weight_last" if tail else "weight_first",
    )(flags, *acts, *grads, s, *([before] if tail else []))


def ring(axis, step):
    n = lax.axis_size(axis)
    return [(i, (i + step) % n) for i in range(n)]


def gather_x(block, first_half, second_half, between=None):
    left = lax.ppermute(block, "x", ring("x", 1))
    right = lax.ppermute(block, "x", ring("x", -1))
    if between is not None:
        left, between = lax.optimization_barrier((left, between))
    far_a = lax.ppermute(first_half(left), "x", ring("x", 1))
    far_b = lax.ppermute(second_half(right), "x", ring("x", -1))
    blocks = (block, left, right, far_a, far_b)
    return blocks if between is None else (blocks, between)


def clips_of_pair():
    def pick(k):
        return lambda b: b.reshape(F, NYH, M * HW, C)[:, k].reshape(POS, C)

    return pick(0), pick(1)


def local(section_inputs, top_grad, norm_gain, norm_shift, conv_weight):
    s = jnp.asarray(shift_matrices(HC), BF)
    wide_s = jnp.asarray(shift_matrices(C), BF)
    x_at = lax.axis_index("x")
    yh = lax.axis_index("yh")
    dp = (x_at * NZ + lax.axis_index("z")) * NYH + yh
    section = lax.axis_index("yl") * 2 + lax.axis_index("c")
    flags = jnp.stack([x_at, yh, section]).astype(jnp.int32)
    swap = ring("yh", 1)

    def mine(value, axis):
        return lax.dynamic_slice_in_dim(value, yh * HC, HC, axis)

    def theirs(value, axis):
        return lax.dynamic_slice_in_dim(value, (1 - yh) * HC, HC, axis)

    def in_order(kept, got, axis):
        return jnp.concatenate([jnp.where(yh == 0, kept, got), jnp.where(yh == 0, got, kept)], axis=axis)

    channel = lax.rem(dp * PART + lax.broadcasted_iota(jnp.int32, (C, PART), 1), C)
    place = (channel == lax.broadcasted_iota(jnp.int32, (C, PART), 0)).astype(BF)
    slots = jnp.dot(place, conv_weight[0], preferred_element_type=F32).astype(BF)
    other = lax.ppermute(theirs(slots, 0), "yh", swap)
    x_in = section_inputs.reshape(POS, C)
    act = forward(x_in, norm_gain, norm_shift)
    other, act = lax.optimization_barrier((other, act))
    window = mine(slots, 0) + other
    chunk = lax.all_to_all(
        jnp.broadcast_to(window[None], (NZ, HC, C)), "z", 0, 0, tiled=True
    ).reshape(SLOTS, C)
    fac = factors(
        flags, mine(x_in, 1), lax.ppermute(theirs(x_in, 1), "yh", swap),
        mine(norm_gain, 1), mine(norm_shift, 1),
    )

    top = top_grad.reshape(M, F, HW, C).transpose(1, 0, 2, 3).reshape(F, 1, M * HW, C)
    both = in_order(top, lax.ppermute(top, "yh", swap), 1).reshape(NYH * POS, C)
    arrived = (mine(both, 1), theirs(both, 1))
    act = act.reshape(F, 1, M * HW, C)
    act = in_order(act, lax.ppermute(act, "yh", swap), 1).reshape(NYH * POS, C)
    kernel_rows, (arrived, fac, act) = gather_x(
        chunk, lambda b: b[: SLOTS // 2], lambda b: b[SLOTS // 2 :], (arrived, fac, act)
    )
    pair_g = both
    for k in range(4):
        if k > 0:
            same, cross = arrived
            both = [jnp.where(yh == 1, cross, same), jnp.where(yh == 1, same, cross)]
            pair_g = jnp.where(section == 3 - k, jnp.concatenate(both, axis=1), pair_g)
        if k == 3:
            arrived = (mine(pair_g, 1), theirs(pair_g, 1))
        sent = conv_back(3 - k, flags, arrived[::-1], s, kernel_rows, fac)
        if k == 1:
            sent, act = lax.optimization_barrier((sent, act))
            acts = gather_x(act, *clips_of_pair())
        if k < 3:
            src, dst = 3 - k, 2 - k
            same = lax.ppermute(sent, ("yl", "c"), [(src, dst)])
            cross = lax.ppermute(
                sent, ("yh", "yl", "c"), [(y * N_PIPE + src, (1 - y) * N_PIPE + dst) for y in range(NYH)]
            )
            arrived = (same, cross)

    pair_dx = sent.reshape(F, NYH, M, HW, HC)
    kept = lax.dynamic_index_in_dim(pair_dx, yh, 1, False)
    given = lax.dynamic_index_in_dim(pair_dx, 1 - yh, 1, False)
    grads, (kept, given) = gather_x(pair_g, *clips_of_pair(), (kept, given))
    got = lax.ppermute(given, "yh", swap)
    dx = in_order(kept, got, -1).transpose(1, 0, 2, 3).reshape(section_inputs.shape)

    partial = weight_back(flags, acts[:3], grads[:3], wide_s)
    partial = weight_back(flags, acts[3:], grads[3:], wide_s, partial)
    parts = lax.all_to_all(partial, "z", 0, 0, tiled=True).reshape(NZ, 1, PART, C)
    return dx, jnp.sum(parts.astype(F32), axis=0)


def solution(mesh):
    fine = Mesh(mesh.devices.reshape(NX, NZ, NYH, 2, 2), ("x", "z", "yh", "yl", "c"))
    dp, pipe = ("x", "z", "yh"), ("yl", "c")
    placed = (
        P(pipe, dp, None, None, None, None, None),
        P(dp, None, None, None, None, None),
        P(pipe, None),
        P(pipe, None),
        P(pipe, dp, None),
    )
    return jax.shard_map(
        local,
        mesh=fine,
        in_specs=placed,
        out_specs=(P(pipe, dp, None, None, None, None, None), P(pipe, dp, None)),
        check_vma=False,
    )
```
